256 devices in a mesh: seq: 32 (over x_lo, z, core), head: 8 (over x_hi, y).
Axes of the slice: x: 4 (x_hi: 2, x_lo: 2; x = x_hi * 2 + x_lo), y: 4, z: 8, core: 2. Of those that a mesh axis runs over, the one named last changes fastest.
Arguments:
- queries: bfloat16 [32768, 4096], P('seq', 'head'), may hold values from -6 to 6
- key_tokens: bfloat16 [32768, 4096], P('seq', 'head'), may hold values from -6 to 6
- value_tokens: bfloat16 [32768, 4096], P('seq', 'head'), may hold values from -6 to 6
- out_weight: bfloat16 [4096, 4096], P('head'), may hold values from -0.09375 to 0.09375
Outputs:
- projected: bfloat16 [32768, 4096], P(('seq', 'head'))
The draws below stay inside these ranges and needn't reach their ends.
All inputs are finite; a program needn't handle non-finite values.
Results may differ from the reference program's by a relative error of at most 0.015.
Values may be sent and summed in bfloat16 or wider, within the bound.
A program may use at most 128 MiB of HBM per device.

```python
import math
import jax
import jax.numpy as jnp
from jax import lax

D = 4096
HEADS = 32
HD = 128
BLK = 256
QG = 16
G1 = 8
WIN = 64
G2 = 32
G3 = 128
G4 = 512
TOKENS = 32768
N_HEAD = 8


def base_draw(key, shape):
    return jnp.clip(jax.random.normal(key, shape, jnp.float32), -4.5, 4.5)


def blocky(key, group_size, width):
    coarse = base_draw(key, (TOKENS // group_size, width))
    return jnp.repeat(coarse, group_size, axis=0)


def layered_field(key, salt):
    width = HEADS * HD
    parts_keys = jax.random.split(jax.random.fold_in(key, salt), 4)
    field = 0.6 * base_draw(parts_keys[0], (TOKENS, width))
    field = field + 0.5 * (blocky(parts_keys[1], G2, width) + blocky(parts_keys[2], G3, width) + blocky(parts_keys[3], G4, width))
    return jnp.clip(field, -5.0, 5.0)


def draw_queries(key, part):
    field = layered_field(key, 11)
    return field.astype(jnp.bfloat16)


def draw_key_tokens(key, part):
    field = layered_field(key, 12)
    return field.astype(jnp.bfloat16)


def draw_value_tokens(key, part):
    return layered_field(key, 13).astype(jnp.bfloat16)


def block_levels(key, shape, shards, smallest, largest):
    loudness = 1.0
    for position, shards_of in shards:
        heights = jax.random.uniform(jax.random.fold_in(jax.random.fold_in(key, 6), position), (shards_of,), jnp.float32, smallest / len(shards), largest / len(shards))
        loudness = loudness * jnp.repeat(jnp.exp(heights), shape[position] // shards_of).reshape((-1,) + (1,) * (len(shape) - 1 - position))
    return loudness


def bell_draw(key, dims, scale, bound, pieces=(), kind=jnp.bfloat16):
    result = jax.random.normal(key, dims, jnp.float32) * scale
    if len(pieces) > 0:
        result = block_levels(key, dims, pieces, -0.22, 0.18) * result
    return jnp.clip(result, min=-bound, max=bound).astype(kind)


def setup_inputs(seed: int = 0) -> dict:
    streams_of = jax.random.split(jax.random.key(seed), 5)
    return {
        "queries": draw_queries(jax.random.fold_in(streams_of[4], 71), 0),
        "key_tokens": draw_key_tokens(jax.random.fold_in(streams_of[4], 71), 0),
        "value_tokens": draw_value_tokens(jax.random.fold_in(streams_of[4], 71), 0),
        "out_weight": bell_draw(streams_of[3], (HEADS * HD, D), (HEADS * HD) ** -0.5, 0.09375, ((0, 8),)),
    }


minus_big = -1e+30

def interp_matrix():
    group_count = BLK // QG
    offsets = jnp.arange(BLK, dtype=jnp.int32)
    numer = 2 * offsets - QG + 1
    lower_idx = jnp.clip(numer // (2 * QG), 0, group_count - 2)
    frac = jnp.clip((numer - lower_idx * 2 * QG).astype(jnp.float32) / (2 * QG), 0.0, 1.0)
    columns = jnp.arange(group_count, dtype=jnp.int32)
    left_part = jnp.where(columns[None, :] == lower_idx[:, None], 1.0 - frac[:, None], 0.0)
    right_part = jnp.where(columns[None, :] == lower_idx[:, None] + 1, frac[:, None], 0.0)
    return (left_part + right_part).astype(jnp.float32)

def level_bounds(block_start):
    first = jnp.maximum(block_start - BLK, 0)
    second = jnp.maximum((first - WIN * G1) // G2 * G2, 0)
    third = jnp.maximum((second - WIN * G2) // G3 * G3, 0)
    fourth = jnp.maximum((third - WIN * G3) // G4 * G4, 0)
    lower = jnp.stack([second, third, fourth, jnp.zeros_like(first)], -1)
    upper = jnp.stack([first, second, third, fourth], -1)
    return (lower, upper)

def reference(queries, key_tokens, value_tokens, out_weight):
    width = HEADS * HD
    score_scale = 1.0 / math.sqrt(HD)
    group_sizes = [G1, G2, G3, G4]
    pooled_k = jnp.concatenate([lax.optimization_barrier(jnp.mean(key_tokens.reshape(TOKENS // size, size, width), axis=1, dtype=jnp.float32)) for size in group_sizes]).astype(jnp.bfloat16)
    pooled_v = jnp.concatenate([lax.optimization_barrier(jnp.mean(value_tokens.reshape(TOKENS // size, size, width), axis=1, dtype=jnp.float32)) for size in group_sizes]).astype(jnp.bfloat16)
    low_end = jnp.concatenate([jnp.arange(TOKENS // size, dtype=jnp.int32) * size for size in group_sizes])
    high_end = jnp.concatenate([jnp.arange(TOKENS // size, dtype=jnp.int32) * size + size for size in group_sizes])
    level_ids = jnp.concatenate([jnp.full((TOKENS // size,), level_id, jnp.int32) for level_id, size in enumerate(group_sizes)])
    far_keys = pooled_k.astype(jnp.float32).reshape(-1, HEADS, HD)
    far_values = pooled_v.astype(jnp.float32).reshape(-1, HEADS, HD)
    zeros_pad = jnp.zeros((BLK, width), jnp.bfloat16)
    ext_k = jnp.concatenate([zeros_pad, key_tokens])
    ext_v = jnp.concatenate([zeros_pad, value_tokens])
    weights_interp = interp_matrix()
    group_count = BLK // QG

    def one_block(index):
        start = index * BLK
        query_block = lax.dynamic_slice_in_dim(queries, start, BLK, 0).astype(jnp.float32).reshape(BLK, HEADS, HD)
        near_keys = lax.dynamic_slice_in_dim(ext_k, start, 2 * BLK, 0).astype(jnp.float32).reshape(2 * BLK, HEADS, HD)
        near_vals = lax.dynamic_slice_in_dim(ext_v, start, 2 * BLK, 0).astype(jnp.float32).reshape(2 * BLK, HEADS, HD)
        scores = jnp.einsum('qhd,khd->hqk', query_block, near_keys) * score_scale
        offsets = jnp.arange(BLK, dtype=jnp.int32)[:, None]
        columns = jnp.arange(2 * BLK, dtype=jnp.int32)[None, :]
        valid = (columns <= offsets + BLK) & (start - BLK + columns >= 0)
        near_max = lax.optimization_barrier(jnp.max(jnp.where(valid, scores, minus_big), axis=-1))
        expo = jnp.where(valid, jnp.exp(scores - near_max[..., None]), 0.0)
        near_den = lax.optimization_barrier(jnp.sum(expo, axis=-1))
        near_w = lax.optimization_barrier(expo.astype(jnp.bfloat16)).astype(jnp.float32)
        near_num = jnp.einsum('hqk,khd->hqd', near_w, near_vals)
        near_out = near_num / near_den[..., None]
        near_lse = near_max + jnp.log(near_den)
        pooled_q = lax.optimization_barrier(jnp.mean(query_block.reshape(group_count, QG, HEADS, HD), axis=1))
        pooled_q = lax.optimization_barrier(pooled_q.astype(jnp.bfloat16)).astype(jnp.float32)
        lower, upper = level_bounds(start)
        chosen = (low_end >= lower[level_ids]) & (high_end <= upper[level_ids])
        far_scores = jnp.einsum('ghd,nhd->hgn', pooled_q, far_keys) * score_scale
        far_max = lax.optimization_barrier(jnp.max(jnp.where(chosen, far_scores, minus_big), axis=-1))
        far_exp = jnp.where(chosen, jnp.exp(far_scores - far_max[..., None]), 0.0)
        far_den = lax.optimization_barrier(jnp.sum(far_exp, axis=-1))
        far_w = lax.optimization_barrier(far_exp.astype(jnp.bfloat16)).astype(jnp.float32)
        far_num = jnp.einsum('hgn,nhd->hgd', far_w, far_values)
        has_far = start - BLK > 0
        safe_den = jnp.where(has_far, far_den, 1.0)
        far_lse = far_max + jnp.log(safe_den)
        far_out = far_num / safe_den[..., None]
        tok_lse = jnp.einsum('rg,hg->hr', weights_interp, far_lse, precision=lax.Precision.HIGHEST)
        tok_out = jnp.einsum('rg,hgd->hrd', weights_interp, far_out, precision=lax.Precision.HIGHEST)
        top_lse = jnp.maximum(near_lse, tok_lse)
        near_weight = jnp.exp(near_lse - top_lse)
        far_weight = jnp.where(has_far, jnp.exp(tok_lse - top_lse), 0.0)
        mixed = (near_weight[..., None] * near_out + far_weight[..., None] * tok_out) / (near_weight + far_weight)[..., None]
        return mixed.transpose(1, 0, 2).reshape(BLK, width).astype(jnp.bfloat16)
    attention = lax.map(one_block, jnp.arange(TOKENS // BLK, dtype=jnp.int32)).reshape(TOKENS, width)
    group_width = width // N_HEAD

    def add_group(total, group_idx):
        cols = lax.dynamic_slice_in_dim(attention, group_idx * group_width, group_width, 1)
        rows_w = lax.dynamic_slice_in_dim(out_weight, group_idx * group_width, group_width, 0)
        part_sum = jnp.dot(cols, rows_w, preferred_element_type=jnp.float32)
        rounded = lax.optimization_barrier(part_sum.astype(jnp.bfloat16)).astype(jnp.float32)
        return (total + rounded, None)
    total, _ = lax.scan(add_group, jnp.zeros((TOKENS, D), jnp.float32), jnp.arange(N_HEAD, dtype=jnp.int32))
    return total.astype(jnp.bfloat16)
```

```python
import functools
import math

import jax
import jax.numpy as jnp
from jax import lax
from jax.experimental import pallas as pl
from jax.experimental.pallas import tpu as pltpu
from jax.sharding import PartitionSpec as P

MESH = pl.DeviceIdType.MESH
HD = 128
BLK = 256
QG = 16
LOG2E = 1.4426950408889634
SCALE2 = LOG2E / math.sqrt(HD)
BIG = -1e30
F32 = jnp.float32
BF16 = jnp.bfloat16

NEAR3 = 3
LAST3 = 11
ROW4 = 288


def iota(shape, dim):
    return lax.broadcasted_iota(jnp.int32, shape, dim)


def dot_nt(a, b):
    return lax.dot_general(a, b, (((1,), (1,)), ((), ())), preferred_element_type=F32)


def dot_nn(a, b):
    return jnp.dot(a, b, preferred_element_type=F32)


def fill_pool_matrix(pm):
    def piece(rows, shift, weight):
        hit = (iota((rows, 1024), 1) >> shift) == iota((rows, 1024), 0)
        return jnp.where(hit, weight, 0.0).astype(BF16)

    pm[0:128, :] = piece(128, 3, 1.0 / 8)
    pm[128:160, :] = piece(32, 5, 1.0 / 32)
    row, col = iota((16, 1024), 0), iota((16, 1024), 1)
    third = jnp.where((col >> 7) == row, 1.0 / 128, 0.0)
    fourth = jnp.where((col >> 9) == (row & 1), 1.0 / 512, 0.0)
    pm[160:176, :] = jnp.where(row < 8, third, fourth).astype(BF16)
    pm[176:240, :] = piece(64, 4, 1.0 / 16)


def fill_interp(wi):
    row, col = iota((BLK, 48), 0), iota((BLK, 48), 1)
    numer = 2 * row - (QG - 1)
    low = jnp.clip(numer >> 5, 0, BLK // QG - 2)
    frac = jnp.clip((numer - low * 32).astype(F32) * (1.0 / 32), 0.0, 1.0)
    group = col & 15
    value = jnp.where(group == low, 1.0 - frac, 0.0) + jnp.where(group == low + 1, frac, 0.0)
    wi[...] = value.astype(BF16)


def bounds(start):
    first = jnp.maximum(start - 256, 0)
    second = jnp.maximum(((first - 512) >> 5) << 5, 0)
    third = jnp.maximum(((second - 2048) >> 7) << 7, 0)
    fourth = jnp.maximum(((third - 8192) >> 9) << 9, 0)
    return first, second, third, fourth


def fill_masks(pick12, pick34, s0):
    shape = (64, 256)
    first, second, third, fourth = bounds(s0 + 256 * (iota(shape, 0) >> 4))
    col = iota(shape, 1)
    is_first = col < 160
    token = jnp.where(is_first, s0 - 768 + 8 * col, s0 - 3072 + 32 * (col - 160))
    size = jnp.where(is_first, 8, 32)
    lower = jnp.where(is_first, second, third)
    upper = jnp.where(is_first, first, second)
    pick12[...] = jnp.where((token >= lower) & (token + size <= upper), 1, 0)
    shape = (64, 640)
    first, second, third, fourth = bounds(s0 + 256 * (iota(shape, 0) >> 4))
    col = iota(shape, 1)
    is_third = col < ROW4
    rest = col - ROW4
    token3 = s0 - LAST3 * 1024 + (col >> 5) * 1024 + (col & 7) * 128
    token4 = s0 - (LAST3 + (rest >> 4)) * 1024 + (rest & 1) * 512
    token = jnp.where(is_third, token3, token4)
    size = jnp.where(is_third, 128, 512)
    head = jnp.where(is_third, (col & 31) >> 3, (rest & 15) >> 1)
    lower = jnp.where(is_third, fourth, 0)
    upper = jnp.where(is_third, third, fourth)
    chosen = (token >= lower) & (token + size <= upper)
    pick34[...] = jnp.where(chosen, head, -1)


def kernel(
    n, q_hbm, k_hbm, v_hbm, att,
    kvx, qs, pm, wi, res, pool12, own34, qp, far12, far34, pick12, pick34, fo, num, mx, den,
    load_sem, send_sem, recv_sem,
):
    me = lax.axis_index("seq")
    s0 = me * 1024

    loads = [
        pltpu.make_async_copy(k_hbm, kvx.at[256:1280, 0:512], load_sem.at[0]),
        pltpu.make_async_copy(v_hbm, kvx.at[256:1280, 512:1024], load_sem.at[1]),
        pltpu.make_async_copy(q_hbm, qs, load_sem.at[2]),
    ]
    for load in loads:
        load.start()

    kvx[0:256, :] = jnp.zeros((256, 1024), BF16)
    far12[...] = jnp.zeros(far12.shape, BF16)
    far34[...] = jnp.zeros(far34.shape, BF16)

    barrier = pltpu.get_barrier_semaphore()

    def greet(k, carry):
        @pl.when(me - k >= 0)
        def _():
            pl.semaphore_signal(barrier, inc=1, device_id={"seq": me - k}, device_id_type=MESH)
        return carry

    lax.fori_loop(1, n, greet, 0)

    fill_pool_matrix(pm)
    for load in loads:
        load.wait()

    def pool(c, carry):
        cols = pl.ds(pl.multiple_of(c * 256, 256), 256)
        res[:, cols] = dot_nn(pm[0:176, :], kvx[256:1280, cols])
        return carry

    lax.fori_loop(0, 4, pool, 0)
    pool12[...] = res[0:160, :].astype(BF16)
    row8 = iota((8, 128), 0)
    sides = []
    for side in range(2):
        tiles = [res[160:168, side * 512 + h * 128 : side * 512 + (h + 1) * 128] for h in range(4)]
        last = jnp.zeros((8, 128), F32)
        for h in range(4):
            lanes = slice(side * 512 + h * 128, side * 512 + (h + 1) * 128)
            last = jnp.where((row8 >> 1) == h, res[168:176, lanes], last)
        sides.append(jnp.concatenate(tiles + [last, jnp.zeros((8, 128), F32)], axis=0))
    own34[...] = jnp.concatenate(sides, axis=1).astype(BF16)
    far12[96:160, :] = pool12[0:64, :]

    @pl.when(me < n - 1)
    def _():
        pl.semaphore_wait(barrier, n - 1 - me)

    def to_later(k, src, dst, slot):
        return pltpu.make_async_remote_copy(
            src_ref=src, dst_ref=dst, send_sem=send_sem.at[slot], recv_sem=recv_sem.at[slot],
            device_id={"seq": lax.rem(me + k, n)}, device_id_type=MESH,
        )

    def copy_tail():
        return to_later(1, kvx.at[1024:1280], kvx.at[0:256], 0)

    def copy1():
        return to_later(1, pool12.at[32:128], far12.at[0:96], 1)

    def copy2(k):
        row = 160 + 32 * (3 - k)
        return to_later(k, pool12.at[128:160], far12.at[row : row + 32], 1 + k)

    def copy3(k):
        row = pl.multiple_of((LAST3 - k) * 32, 32)
        return to_later(k, own34.at[0:32], far34.at[pl.ds(row, 32)], 5 + k - NEAR3)

    def copy4(k):
        row = pl.multiple_of(ROW4 + (k - LAST3) * 16, 16)
        return to_later(k, own34.at[32:48], far34.at[pl.ds(row, 16)], 14 + k - LAST3)

    def each(apply, condition):
        @pl.when(condition(1))
        def _():
            apply(copy1())
        for k in (1, 2, 3):
            @pl.when(condition(k))
            def _():
                apply(copy2(k))

        def third(k, carry):
            @pl.when(condition(k))
            def _():
                apply(copy3(k))
            return carry

        def fourth(k, carry):
            @pl.when(condition(k))
            def _():
                apply(copy4(k))
            return carry

        lax.fori_loop(NEAR3, LAST3 + 1, third, 0)
        lax.fori_loop(LAST3, n, fourth, 0)

    has_later = lambda k: me + k < n
    has_earlier = lambda k: me - k >= 0

    @pl.when(has_later(1))
    def _():
        copy_tail().start()

    each(lambda copy: copy.start(), has_later)

    qp[...] = dot_nn(pm[176:240, :], qs[...]).astype(BF16)
    fill_interp(wi)
    fill_masks(pick12, pick34, s0)

    def near(b, h):
        rows = pl.ds(pl.multiple_of(b * 256, 256), 256)
        next_rows = pl.ds(pl.multiple_of(b * 256 + 256, 256), 256)
        lanes = pl.ds(pl.multiple_of(h * 128, 128), 128)
        vlanes = pl.ds(pl.multiple_of(512 + h * 128, 128), 128)
        q = qs[rows, lanes]
        s_prev = dot_nt(q, kvx[rows, lanes])
        s_own = dot_nt(q, kvx[next_rows, lanes])
        s_prev = jnp.where(s0 + b * 256 > 0, s_prev, BIG)
        s_own = jnp.where(iota((256, 256), 1) <= iota((256, 256), 0), s_own, BIG)
        top = jnp.max(jnp.maximum(s_prev, s_own), axis=1, keepdims=True) * SCALE2
        w_prev = jnp.exp2(s_prev * SCALE2 - top)
        w_own = jnp.exp2(s_own * SCALE2 - top)
        total = jnp.sum(w_prev + w_own, axis=1, keepdims=True)
        num[rows, lanes] = dot_nn(w_prev.astype(BF16), kvx[rows, vlanes]) + dot_nn(
            w_own.astype(BF16), kvx[next_rows, vlanes]
        )
        mx[rows, lanes] = jnp.broadcast_to(top, (256, 128))
        den[rows, lanes] = jnp.broadcast_to(total, (256, 128))

    def near_step(i, carry):
        near(i >> 2, i & 3)
        return carry

    lax.fori_loop(4, 16, near_step, 0)

    @pl.when(has_earlier(1))
    def _():
        copy_tail().wait_recv()

    lax.fori_loop(0, 4, near_step, 0)

    each(lambda copy: copy.wait_recv(), has_earlier)

    def far(h, carry):
        lanes = pl.ds(pl.multiple_of(h * 128, 128), 128)
        vlanes = pl.ds(pl.multiple_of(512 + h * 128, 128), 128)
        pooled = qp[:, lanes]
        in12 = pick12[...] > 0
        in34 = pick34[...] == h
        s12 = jnp.where(in12, dot_nt(pooled, far12[:, lanes]), BIG)
        s34 = jnp.where(in34, dot_nt(pooled, far34[:, 0:128]), BIG)
        top = jnp.maximum(jnp.max(s12, axis=1, keepdims=True), jnp.max(s34, axis=1, keepdims=True)) * SCALE2
        w12 = jnp.where(in12, jnp.exp2(s12 * SCALE2 - top), 0.0)
        w34 = jnp.where(in34, jnp.exp2(s34 * SCALE2 - top), 0.0)
        total = jnp.sum(w12, axis=1, keepdims=True) + jnp.sum(w34, axis=1, keepdims=True)
        acc = dot_nn(w12.astype(BF16), far12[:, vlanes]) + dot_nn(w34.astype(BF16), far34[:, 128:256])
        some = total > 0
        safe = jnp.where(some, total, 1.0)
        lse = jnp.where(some, top + jnp.log(safe) * LOG2E, BIG)
        both = jnp.concatenate([acc / safe, jnp.broadcast_to(lse, (64, 128))], axis=1)
        high = both.astype(BF16)
        rest = both - high.astype(F32)
        middle = rest.astype(BF16)
        low = (rest - middle.astype(F32)).astype(BF16)
        for b in range(4):
            for j, part in enumerate((high, middle, low)):
                fo[h * 4 + b, 16 * j : 16 * (j + 1), :] = part[16 * b : 16 * (b + 1), :]
        return carry

    lax.fori_loop(0, 4, far, 0)

    def mix(i, carry):
        b, h = i >> 2, i & 3
        rows = pl.ds(pl.multiple_of(b * 256, 256), 256)
        lanes = pl.ds(pl.multiple_of(h * 128, 128), 128)
        tok = dot_nn(wi[...], fo[h * 4 + b])
        tok_out, tok_lse = tok[:, 0:128], tok[:, 128:256]
        near_max = mx[rows, lanes]
        top = jnp.maximum(near_max, tok_lse)
        a = jnp.exp2(near_max - top)
        b_far = jnp.exp2(tok_lse - top)
        mixed = (num[rows, lanes] * a + tok_out * b_far) / (den[rows, lanes] * a + b_far)
        att[rows, lanes] = mixed.astype(BF16)
        return carry

    lax.fori_loop(0, 16, mix, 0)

    @pl.when(has_later(1))
    def _():
        copy_tail().wait_send()

    each(lambda copy: copy.wait_send(), has_later)


def attention(n, q, k, v):
    any_spec = pl.BlockSpec(memory_space=pl.ANY)
    vm = pltpu.VMEM
    return pl.pallas_call(
        functools.partial(kernel, n),
        out_shape=jax.ShapeDtypeStruct(q.shape, BF16),
        in_specs=[any_spec] * 3,
        out_specs=pl.BlockSpec(memory_space=pltpu.VMEM),
        scratch_shapes=[
            vm((1280, 1024), BF16),
            vm((1024, 512), BF16),
            vm((240, 1024), BF16),
            vm((256, 48), BF16),
            vm((176, 1024), F32),
            vm((160, 1024), BF16),
            vm((48, 256), BF16),
            vm((64, 512), BF16),
            vm((256, 1024), BF16),
            vm((640, 256), BF16),
            vm((64, 256), jnp.int32),
            vm((64, 640), jnp.int32),
            vm((16, 48, 256), BF16),
            vm((1024, 512), F32),
            vm((1024, 512), F32),
            vm((1024, 512), F32),
            pltpu.SemaphoreType.DMA((3,)),
            pltpu.SemaphoreType.DMA((35,)),
            pltpu.SemaphoreType.DMA((35,)),
        ],
        compiler_params=pltpu.CompilerParams(
            collective_id=0, has_side_effects=True, vmem_limit_bytes=48 * 1024 * 1024
        ),
        cost_estimate=pl.CostEstimate(flops=2 * 10**9, bytes_accessed=4 * 2**20, transcendentals=2 * 10**6),
    )(q, k, v)


def solution(mesh):
    n = mesh.shape["seq"]

    def body(queries, key_tokens, value_tokens, out_weight):
        att = attention(n, queries, key_tokens, value_tokens)
        share = jnp.dot(att, out_weight, preferred_element_type=F32).astype(BF16)
        return lax.psum_scatter(share, "head", scatter_dimension=0, tiled=True)

    in_specs = (P("seq", "head"), P("seq", "head"), P("seq", "head"), P("head", None))
    out_specs = P(("seq", "head"), None)
    return jax.shard_map(body, mesh=mesh, in_specs=in_specs, out_specs=out_specs, check_vma=False)
```

```python
import functools
import math

import jax
import jax.numpy as jnp
from jax import lax
from jax.experimental import pallas as pl
from jax.experimental.pallas import tpu as pltpu
from jax.sharding import PartitionSpec as P

MESH = pl.DeviceIdType.MESH
HD = 128
BLK = 256
QG = 16
LOG2E = 1.4426950408889634
SCALE2 = LOG2E / math.sqrt(HD)
BIG = -1e30
F32 = jnp.float32
BF16 = jnp.bfloat16

NEAR3 = 3
LAST3 = 11
ROW4 = 288


def iota(shape, dim):
    return lax.broadcasted_iota(jnp.int32, shape, dim)


def dot_nt(a, b):
    return lax.dot_general(a, b, (((1,), (1,)), ((), ())), preferred_element_type=F32)


def dot_nn(a, b):
    return jnp.dot(a, b, preferred_element_type=F32)


def fill_pool_matrix(pm):
    def piece(rows, shift, weight):
        hit = (iota((rows, 1024), 1) >> shift) == iota((rows, 1024), 0)
        return jnp.where(hit, weight, 0.0).astype(BF16)

    pm[0:128, :] = piece(128, 3, 1.0 / 8)
    pm[128:160, :] = piece(32, 5, 1.0 / 32)
    row, col = iota((16, 1024), 0), iota((16, 1024), 1)
    third = jnp.where((col >> 7) == row, 1.0 / 128, 0.0)
    fourth = jnp.where((col >> 9) == (row & 1), 1.0 / 512, 0.0)
    pm[160:176, :] = jnp.where(row < 8, third, fourth).astype(BF16)
    pm[176:240, :] = piece(64, 4, 1.0 / 16)


def fill_interp(wi):
    row, col = iota((BLK, 48), 0), iota((BLK, 48), 1)
    numer = 2 * row - (QG - 1)
    low = jnp.clip(numer >> 5, 0, BLK // QG - 2)
    frac = jnp.clip((numer - low * 32).astype(F32) * (1.0 / 32), 0.0, 1.0)
    group = col & 15
    value = jnp.where(group == low, 1.0 - frac, 0.0) + jnp.where(group == low + 1, frac, 0.0)
    wi[...] = value.astype(BF16)


def bounds(start):
    first = jnp.maximum(start - 256, 0)
    second = jnp.maximum(((first - 512) >> 5) << 5, 0)
    third = jnp.maximum(((second - 2048) >> 7) << 7, 0)
    fourth = jnp.maximum(((third - 8192) >> 9) << 9, 0)
    return first, second, third, fourth


def fill_masks(pick12, pick34, s0):
    shape = (64, 256)
    first, second, third, fourth = bounds(s0 + 256 * (iota(shape, 0) >> 4))
    col = iota(shape, 1)
    is_first = col < 160
    token = jnp.where(is_first, s0 - 768 + 8 * col, s0 - 3072 + 32 * (col - 160))
    size = jnp.where(is_first, 8, 32)
    lower = jnp.where(is_first, second, third)
    upper = jnp.where(is_first, first, second)
    pick12[...] = jnp.where((token >= lower) & (token + size <= upper), 1, 0)
    shape = (64, 640)
    first, second, third, fourth = bounds(s0 + 256 * (iota(shape, 0) >> 4))
    col = iota(shape, 1)
    is_third = col < ROW4
    rest = col - ROW4
    token3 = s0 - LAST3 * 1024 + (col >> 5) * 1024 + (col & 7) * 128
    token4 = s0 - (LAST3 + (rest >> 4)) * 1024 + (rest & 1) * 512
    token = jnp.where(is_third, token3, token4)
    size = jnp.where(is_third, 128, 512)
    head = jnp.where(is_third, (col & 31) >> 3, (rest & 15) >> 1)
    lower = jnp.where(is_third, fourth, 0)
    upper = jnp.where(is_third, third, fourth)
    chosen = (token >= lower) & (token + size <= upper)
    pick34[...] = jnp.where(chosen, head, -1)


def kernel(
    n, q_hbm, k_hbm, v_hbm, w_hbm, out,
    kvx, qs, pm, wi, res, pool12, own34, qp, far12, far34, pick12, pick34, fo, num, mx, den,
    att, att_in, w_own, w_in, sb1, rb1, sb2, rb2, own,
    load_sem, send_sem, recv_sem, att_send, att_recv, w_send, w_recv, send1, recv1, send2, recv2,
):
    me = lax.axis_index("seq")
    head = lax.axis_index("head")
    s0 = me * 1024
    half = lax.div(head, 4)
    y = lax.rem(head, 4)
    partner = lax.rem(head + 4, 8)
    up = half * 4 + lax.rem(y + 1, 4)
    down = half * 4 + lax.rem(y + 3, 4)
    across = {"seq": lax.rem(me + n // 2, n), "head": partner}
    quarter = lax.rem(me, 4)
    sibling = me + 1 - 2 * lax.rem(me, 2)
    beside = me + 2 - 4 * lax.div(quarter, 2)

    loads = [
        pltpu.make_async_copy(k_hbm, kvx.at[256:1280, 0:512], load_sem.at[0]),
        pltpu.make_async_copy(v_hbm, kvx.at[256:1280, 512:1024], load_sem.at[1]),
        pltpu.make_async_copy(q_hbm, qs, load_sem.at[2]),
    ]
    load_w = pltpu.make_async_copy(w_hbm, w_own, load_sem.at[3])
    for load in loads:
        load.start()

    kvx[0:256, :] = jnp.zeros((256, 1024), BF16)
    far12[...] = jnp.zeros(far12.shape, BF16)
    far34[...] = jnp.zeros(far34.shape, BF16)

    barrier = pltpu.get_barrier_semaphore()

    def greet(k, carry):
        @pl.when(me - k >= 0)
        def _():
            pl.semaphore_signal(barrier, inc=1, device_id={"seq": me - k}, device_id_type=MESH)
        return carry

    lax.fori_loop(1, n, greet, 0)
    for place in ({"head": partner}, {"head": up}, {"head": down}, across, {"seq": sibling}, {"seq": beside}):
        pl.semaphore_signal(barrier, inc=1, device_id=place, device_id_type=MESH)

    fill_pool_matrix(pm)
    for load in loads:
        load.wait()

    def pool(c, carry):
        cols = pl.ds(pl.multiple_of(c * 256, 256), 256)
        res[:, cols] = dot_nn(pm[0:176, :], kvx[256:1280, cols])
        return carry

    lax.fori_loop(0, 4, pool, 0)
    pool12[...] = res[0:160, :].astype(BF16)
    row8 = iota((8, 128), 0)
    sides = []
    for side in range(2):
        tiles = [res[160:168, side * 512 + h * 128 : side * 512 + (h + 1) * 128] for h in range(4)]
        last = jnp.zeros((8, 128), F32)
        for h in range(4):
            lanes = slice(side * 512 + h * 128, side * 512 + (h + 1) * 128)
            last = jnp.where((row8 >> 1) == h, res[168:176, lanes], last)
        sides.append(jnp.concatenate(tiles + [last, jnp.zeros((8, 128), F32)], axis=0))
    own34[...] = jnp.concatenate(sides, axis=1).astype(BF16)
    far12[96:160, :] = pool12[0:64, :]

    pl.semaphore_wait(barrier, n - 1 - me + 6)
    load_w.start()

    def to_later(k, src, dst, slot):
        return pltpu.make_async_remote_copy(
            src_ref=src, dst_ref=dst, send_sem=send_sem.at[slot], recv_sem=recv_sem.at[slot],
            device_id={"seq": lax.rem(me + k, n)}, device_id_type=MESH,
        )

    def copy_tail():
        return to_later(1, kvx.at[1024:1280], kvx.at[0:256], 0)

    def copy1():
        return to_later(1, pool12.at[32:128], far12.at[0:96], 1)

    def copy2(k):
        row = 160 + 32 * (3 - k)
        return to_later(k, pool12.at[128:160], far12.at[row : row + 32], 1 + k)

    def copy3(k):
        row = pl.multiple_of((LAST3 - k) * 32, 32)
        return to_later(k, own34.at[0:32], far34.at[pl.ds(row, 32)], 5 + k - NEAR3)

    def copy4(k):
        row = pl.multiple_of(ROW4 + (k - LAST3) * 16, 16)
        return to_later(k, own34.at[32:48], far34.at[pl.ds(row, 16)], 14 + k - LAST3)

    def each(apply, condition):
        @pl.when(condition(1))
        def _():
            apply(copy1())
        for k in (1, 2, 3):
            @pl.when(condition(k))
            def _():
                apply(copy2(k))

        def third(k, carry):
            @pl.when(condition(k))
            def _():
                apply(copy3(k))
            return carry

        def fourth(k, carry):
            @pl.when(condition(k))
            def _():
                apply(copy4(k))
            return carry

        lax.fori_loop(NEAR3, LAST3 + 1, third, 0)
        lax.fori_loop(LAST3, n, fourth, 0)

    has_later = lambda k: me + k < n
    has_earlier = lambda k: me - k >= 0

    @pl.when(has_later(1))
    def _():
        copy_tail().start()

    each(lambda copy: copy.start(), has_later)

    def w_copy(src, kind, j, rows_of, place):
        rows = pl.ds(pl.multiple_of(rows_of * 128, 128), 128)
        cols = pl.ds(pl.multiple_of(j * 1024, 1024), 1024)
        return pltpu.make_async_remote_copy(
            src_ref=src.at[rows, cols], dst_ref=w_in.at[rows, cols],
            send_sem=w_send.at[kind * 4 + j], recv_sem=w_recv.at[kind * 4 + j],
            device_id=place, device_id_type=MESH,
        )

    other = lax.rem(quarter + 2, 4)
    w_across = lambda j: w_copy(w_hbm, 0, j, quarter, across)
    w_sibling = lambda j: w_copy(w_in, 1, j, quarter, {"seq": sibling})
    w_beside = lambda j: w_copy(w_in, 2, j, quarter, {"seq": beside})
    w_last = lambda j: w_copy(w_in, 3, j, other, {"seq": sibling})

    def pass_on(j):
        w_across(j).wait_recv()
        w_sibling(j).start()
        w_beside(j).start()

    def pass_last(j):
        w_beside(j).wait_recv()
        w_last(j).start()

    for j in range(4):
        w_across(j).start()

    qp[...] = dot_nn(pm[176:240, :], qs[...]).astype(BF16)
    fill_interp(wi)
    fill_masks(pick12, pick34, s0)

    def near(b, h):
        rows = pl.ds(pl.multiple_of(b * 256, 256), 256)
        next_rows = pl.ds(pl.multiple_of(b * 256 + 256, 256), 256)
        lanes = pl.ds(pl.multiple_of(h * 128, 128), 128)
        vlanes = pl.ds(pl.multiple_of(512 + h * 128, 128), 128)
        q = qs[rows, lanes]
        s_prev = dot_nt(q, kvx[rows, lanes])
        s_own = dot_nt(q, kvx[next_rows, lanes])
        s_prev = jnp.where(s0 + b * 256 > 0, s_prev, BIG)
        s_own = jnp.where(iota((256, 256), 1) <= iota((256, 256), 0), s_own, BIG)
        top = jnp.max(jnp.maximum(s_prev, s_own), axis=1, keepdims=True) * SCALE2
        w_prev = jnp.exp2(s_prev * SCALE2 - top)
        w_own = jnp.exp2(s_own * SCALE2 - top)
        total = jnp.sum(w_prev + w_own, axis=1, keepdims=True)
        num[rows, lanes] = dot_nn(w_prev.astype(BF16), kvx[rows, vlanes]) + dot_nn(
            w_own.astype(BF16), kvx[next_rows, vlanes]
        )
        mx[rows, lanes] = jnp.broadcast_to(top, (256, 128))
        den[rows, lanes] = jnp.broadcast_to(total, (256, 128))

    def near_step(i, carry):
        near(i >> 2, i & 3)
        return carry

    lax.fori_loop(4, 16, near_step, 0)
    pass_on(0)

    @pl.when(has_earlier(1))
    def _():
        copy_tail().wait_recv()

    lax.fori_loop(0, 4, near_step, 0)

    each(lambda copy: copy.wait_recv(), has_earlier)

    def far(h, carry):
        lanes = pl.ds(pl.multiple_of(h * 128, 128), 128)
        vlanes = pl.ds(pl.multiple_of(512 + h * 128, 128), 128)
        pooled = qp[:, lanes]
        in12 = pick12[...] > 0
        in34 = pick34[...] == h
        s12 = jnp.where(in12, dot_nt(pooled, far12[:, lanes]), BIG)
        s34 = jnp.where(in34, dot_nt(pooled, far34[:, 0:128]), BIG)
        top = jnp.maximum(jnp.max(s12, axis=1, keepdims=True), jnp.max(s34, axis=1, keepdims=True)) * SCALE2
        w12 = jnp.where(in12, jnp.exp2(s12 * SCALE2 - top), 0.0)
        w34 = jnp.where(in34, jnp.exp2(s34 * SCALE2 - top), 0.0)
        total = jnp.sum(w12, axis=1, keepdims=True) + jnp.sum(w34, axis=1, keepdims=True)
        acc = dot_nn(w12.astype(BF16), far12[:, vlanes]) + dot_nn(w34.astype(BF16), far34[:, 128:256])
        some = total > 0
        safe = jnp.where(some, total, 1.0)
        lse = jnp.where(some, top + jnp.log(safe) * LOG2E, BIG)
        both = jnp.concatenate([acc / safe, jnp.broadcast_to(lse, (64, 128))], axis=1)
        high = both.astype(BF16)
        rest = both - high.astype(F32)
        middle = rest.astype(BF16)
        low = (rest - middle.astype(F32)).astype(BF16)
        for b in range(4):
            for j, part in enumerate((high, middle, low)):
                fo[h * 4 + b, 16 * j : 16 * (j + 1), :] = part[16 * b : 16 * (b + 1), :]
        return carry

    lax.fori_loop(0, 4, far, 0)

    pass_on(1)
    pass_last(0)

    def mix(b):
        rows = pl.ds(pl.multiple_of(b * 256, 256), 256)

        def one(h, carry):
            lanes = pl.ds(pl.multiple_of(h * 128, 128), 128)
            tok = dot_nn(wi[...], fo[h * 4 + b])
            tok_out, tok_lse = tok[:, 0:128], tok[:, 128:256]
            near_max = mx[rows, lanes]
            top = jnp.maximum(near_max, tok_lse)
            a = jnp.exp2(near_max - top)
            b_far = jnp.exp2(tok_lse - top)
            mixed = (num[rows, lanes] * a + tok_out * b_far) / (den[rows, lanes] * a + b_far)
            att[rows, lanes] = mixed.astype(BF16)
            return carry

        lax.fori_loop(0, 4, one, 0)

    def give(i):
        row = pl.multiple_of((1 - half) * 512 + i * 256, 256)
        return pltpu.make_async_remote_copy(
            src_ref=att.at[pl.ds(row, 256)], dst_ref=att_in.at[i * 256 : i * 256 + 256],
            send_sem=att_send.at[i], recv_sem=att_recv.at[i],
            device_id={"head": partner}, device_id_type=MESH,
        )

    for i in range(2):
        mix((1 - half) * 2 + i)
        give(i).start()
    pass_on(2)
    pass_last(1)
    for i in range(2):
        mix(half * 2 + i)
    load_w.wait()
    for i in range(2):
        give(i).wait_recv()

    def share(target, chunk):
        own_rows = pl.ds(pl.multiple_of(half * 512 + target * 128, 128), 128)
        in_rows = pl.ds(pl.multiple_of(target * 128, 128), 128)
        cols = pl.ds(pl.multiple_of(chunk * 512, 512), 512)
        return dot_nn(att[own_rows, :], w_own[:, cols]) + dot_nn(att_in[in_rows, :], w_in[:, cols])

    def first_copy(side, j):
        slot = side * 4 + j
        return pltpu.make_async_remote_copy(
            src_ref=sb1.at[slot], dst_ref=rb1.at[slot], send_sem=send1.at[slot], recv_sem=recv1.at[slot],
            device_id={"head": (up, down)[side]}, device_id_type=MESH,
        )

    def second_copy(side, chunk):
        slot = side * 8 + chunk
        return pltpu.make_async_remote_copy(
            src_ref=sb2.at[slot], dst_ref=rb2.at[slot], send_sem=send2.at[slot], recv_sem=recv2.at[slot],
            device_id={"head": (up, down)[side]}, device_id_type=MESH,
        )

    y_up, y_down, y_far = lax.rem(y + 1, 4), lax.rem(y + 3, 4), lax.rem(y + 2, 4)

    def begin(j, carry):
        w_sibling(j).wait_recv()
        w_last(j).wait_recv()
        for side in range(2):
            sb1[side * 4 + j] = share(y_far, 2 * j + side).astype(BF16)
            first_copy(side, j).start()
        for side in range(2):
            chunk = 2 * j + 1 - side
            sb2[side * 8 + chunk] = share((y_up, y_down)[side], chunk).astype(BF16)
            second_copy(side, chunk).start()
        return carry

    lax.fori_loop(0, 1, begin, 0)
    pass_on(3)
    pass_last(2)
    lax.fori_loop(1, 2, begin, 0)
    pass_last(3)
    lax.fori_loop(2, 4, begin, 0)

    def follow(j, carry):
        for side in range(2):
            chunk = 2 * j + side
            mine = share((y_up, y_down)[side], chunk)
            first_copy(side, j).wait_recv()
            sb2[side * 8 + chunk] = (mine + rb1[side * 4 + j].astype(F32)).astype(BF16)
            second_copy(side, chunk).start()
        return carry

    lax.fori_loop(0, 4, follow, 0)

    def keep(chunk, carry):
        own[chunk] = share(y, chunk)
        return carry

    lax.fori_loop(0, 8, keep, 0)

    def finish(chunk, carry):
        for side in range(2):
            second_copy(side, chunk).wait_recv()
        total = own[chunk] + rb2[chunk].astype(F32) + rb2[8 + chunk].astype(F32)
        out[:, pl.ds(pl.multiple_of(chunk * 512, 512), 512)] = total.astype(BF16)
        return carry

    lax.fori_loop(0, 8, finish, 0)

    @pl.when(has_later(1))
    def _():
        copy_tail().wait_send()

    each(lambda copy: copy.wait_send(), has_later)
    for j in range(4):
        w_across(j).wait_send()
        w_sibling(j).wait_send()
        w_beside(j).wait_send()
        w_last(j).wait_send()
        for side in range(2):
            first_copy(side, j).wait_send()
            second_copy(side, j).wait_send()
            second_copy(side, 4 + j).wait_send()
    for i in range(2):
        give(i).wait_send()


def layer(n, q, k, v, w):
    hbm_spec = pl.BlockSpec(memory_space=pltpu.HBM)
    vm = pltpu.VMEM
    return pl.pallas_call(
        functools.partial(kernel, n),
        out_shape=jax.ShapeDtypeStruct((128, 4096), BF16),
        in_specs=[hbm_spec] * 4,
        out_specs=pl.BlockSpec(memory_space=pltpu.VMEM),
        scratch_shapes=[
            vm((1280, 1024), BF16),
            vm((1024, 512), BF16),
            vm((240, 1024), BF16),
            vm((256, 48), BF16),
            vm((176, 1024), F32),
            vm((160, 1024), BF16),
            vm((48, 256), BF16),
            vm((64, 512), BF16),
            vm((256, 1024), BF16),
            vm((640, 256), BF16),
            vm((64, 256), jnp.int32),
            vm((64, 640), jnp.int32),
            vm((16, 48, 256), BF16),
            vm((1024, 512), F32),
            vm((1024, 512), F32),
            vm((1024, 512), F32),
            vm((1024, 512), BF16),
            vm((512, 512), BF16),
            vm((512, 4096), BF16),
            vm((512, 4096), BF16),
            vm((8, 128, 512), BF16),
            vm((8, 128, 512), BF16),
            vm((16, 128, 512), BF16),
            vm((16, 128, 512), BF16),
            vm((8, 128, 512), F32),
            pltpu.SemaphoreType.DMA((4,)),
        ]
        + [pltpu.SemaphoreType.DMA((count,)) for count in (35, 35, 2, 2, 16, 16, 8, 8, 16, 16)],
        compiler_params=pltpu.CompilerParams(
            collective_id=0, has_side_effects=True, vmem_limit_bytes=56 * 1024 * 1024
        ),
        cost_estimate=pl.CostEstimate(flops=6 * 10**9, bytes_accessed=8 * 2**20, transcendentals=2 * 10**6),
    )(q, k, v, w)


def solution(mesh):
    n = mesh.shape["seq"]

    def body(queries, key_tokens, value_tokens, out_weight):
        return layer(n, queries, key_tokens, value_tokens, out_weight)

    in_specs = (P("seq", "head"), P("seq", "head"), P("seq", "head"), P("head", None))
    out_specs = P(("seq", "head"), None)
    return jax.shard_map(body, mesh=mesh, in_specs=in_specs, out_specs=out_specs, check_vma=False)
```

```python
import functools
import math

import jax
import jax.numpy as jnp
from jax import lax
from jax.experimental import pallas as pl
from jax.experimental.pallas import tpu as pltpu
from jax.sharding import PartitionSpec as P

MESH = pl.DeviceIdType.MESH
HD = 128
BLK = 256
QG = 16
LOG2E = 1.4426950408889634
SCALE2 = LOG2E / math.sqrt(HD)
BIG = -1e30
F32 = jnp.float32
BF16 = jnp.bfloat16

BACK3 = 6
STRIDE3 = 704


def iota(shape, dim):
    return lax.broadcasted_iota(jnp.int32, shape, dim)


def dot_nt(a, b):
    return lax.dot_general(a, b, (((1,), (1,)), ((), ())), preferred_element_type=F32)


def dot_nn(a, b):
    return jnp.dot(a, b, preferred_element_type=F32)


def fill_pool_matrix(pm):
    def piece(rows, shift, weight):
        hit = (iota((rows, 1024), 1) >> shift) == iota((rows, 1024), 0)
        return jnp.where(hit, weight, 0.0).astype(BF16)

    pm[0:128, :] = piece(128, 3, 1.0 / 8)
    pm[128:160, :] = piece(32, 5, 1.0 / 32)
    row, col = iota((16, 1024), 0), iota((16, 1024), 1)
    third = jnp.where((col >> 7) == row, 1.0 / 128, 0.0)
    fourth = jnp.where((col >> 9) == (row & 1), 1.0 / 512, 0.0)
    pm[160:176, :] = jnp.where(row < 8, third, fourth).astype(BF16)
    pm[176:240, :] = piece(64, 4, 1.0 / 16)


def fill_interp(wi):
    row, col = iota((BLK, 48), 0), iota((BLK, 48), 1)
    numer = 2 * row - (QG - 1)
    low = jnp.clip(numer >> 5, 0, BLK // QG - 2)
    frac = jnp.clip((numer - low * 32).astype(F32) * (1.0 / 32), 0.0, 1.0)
    group = col & 15
    value = jnp.where(group == low, 1.0 - frac, 0.0) + jnp.where(group == low + 1, frac, 0.0)
    wi[...] = value.astype(BF16)


def bounds(start):
    first = jnp.maximum(start - 256, 0)
    second = jnp.maximum(((first - 512) >> 5) << 5, 0)
    third = jnp.maximum(((second - 2048) >> 7) << 7, 0)
    fourth = jnp.maximum(((third - 8192) >> 9) << 9, 0)
    return first, second, third, fourth


def fill_masks(pick12, pick3, pick4, s0):
    shape = (64, 256)
    first, second, third, fourth = bounds(s0 + 256 * (iota(shape, 0) >> 4))
    col = iota(shape, 1)
    is_first = col < 160
    token = jnp.where(is_first, s0 - 768 + 8 * col, s0 - 3072 + 32 * (col - 160))
    size = jnp.where(is_first, 8, 32)
    lower = jnp.where(is_first, second, third)
    upper = jnp.where(is_first, first, second)
    pick12[...] = jnp.where((token >= lower) & (token + size <= upper), 1, 0)
    shape = (64, 384)
    first, second, third, fourth = bounds(s0 + 256 * (iota(shape, 0) >> 4))
    col = iota(shape, 1)
    core = jnp.where(col < 192, 0, 1)
    rest = col - 192 * core
    token = ((s0 >> 11) - BACK3 + (rest >> 5)) * 2048 + core * 1024 + (rest & 7) * 128
    chosen = (token >= fourth) & (token + 128 <= third)
    pick3[...] = jnp.where(chosen, (rest & 31) >> 3, -1)
    token = (rest >> 4) * 2048 + core * 1024 + (rest & 1) * 512
    chosen = (token >= 0) & (token + 512 <= fourth)
    pick4[...] = jnp.where(chosen, (rest & 15) >> 1, -1)


def kernel(
    n, q_hbm, k_hbm, v_hbm, w_hbm, out,
    kvx, qs, pm, wi, res, pool12, qp, far12, far3, far4, pick12, pick3, pick4, fo, num, mx, den,
    att, att_in, w_own, w_in, sb1, rb1, sb2, rb2, own,
    load_sem, near_send, near_recv, peer_send, peer_recv, side_send, side_recv,
    att_send, att_recv, w_send, w_recv, send1, recv1, send2, recv2,
):
    me = lax.axis_index("seq")
    head = lax.axis_index("head")
    s0 = me * 1024
    chips = n // 2
    row_chips = chips // 2
    core = lax.rem(me, 2)
    chip = lax.div(me, 2)
    x_low = lax.div(chip, row_chips)
    z = lax.rem(chip, row_chips)
    half = lax.div(head, 4)
    y = lax.rem(head, 4)
    partner = lax.rem(head + 4, 8)
    up = half * 4 + lax.rem(y + 1, 4)
    down = half * 4 + lax.rem(y + 3, 4)
    x_next = lax.rem(me + chips, n)
    across = {"seq": x_next, "head": partner}
    quarter = lax.rem(me, 4)
    sibling = me + 1 - 2 * core
    beside = me + 2 - 4 * lax.div(quarter, 2)

    def z_peer(d):
        return x_low * chips + lax.rem(z + d, row_chips) * 2 + core

    loads = [
        pltpu.make_async_copy(k_hbm, kvx.at[256:1280, 0:512], load_sem.at[0]),
        pltpu.make_async_copy(v_hbm, kvx.at[256:1280, 512:1024], load_sem.at[1]),
        pltpu.make_async_copy(q_hbm, qs, load_sem.at[2]),
    ]
    load_w = pltpu.make_async_copy(w_hbm, w_own, load_sem.at[3])
    for load in loads:
        load.start()

    for c in range(2):
        far3[c * STRIDE3 : c * STRIDE3 + BACK3 * 32, :] = jnp.zeros((BACK3 * 32, 256), BF16)
        far4[c * 256 + 128 : c * 256 + 256, :] = jnp.zeros((128, 256), BF16)

    barrier = pltpu.get_barrier_semaphore()
    places = [{"seq": z_peer(d)} for d in range(1, row_chips)]
    places += [{"seq": lax.rem(me + n - k, n)} for k in (1, 2, 3)]
    places += [{"seq": sibling}, {"seq": x_next}, {"head": partner}, {"head": up}, {"head": down}, across]
    for place in places:
        pl.semaphore_signal(barrier, inc=1, device_id=place, device_id_type=MESH)

    fill_pool_matrix(pm)
    for load in loads:
        load.wait()
    load_w.start()

    def pool(c, carry):
        cols = pl.ds(pl.multiple_of(c * 256, 256), 256)
        res[:, cols] = dot_nn(pm[0:176, :], kvx[256:1280, cols])
        return carry

    lax.fori_loop(0, 4, pool, 0)
    pool12[...] = res[0:160, :].astype(BF16)
    row8 = iota((8, 128), 0)
    sides3, sides4 = [], []
    for side in range(2):
        tiles = [res[160:168, side * 512 + h * 128 : side * 512 + (h + 1) * 128] for h in range(4)]
        last = jnp.zeros((8, 128), F32)
        for h in range(4):
            lanes = slice(side * 512 + h * 128, side * 512 + (h + 1) * 128)
            last = jnp.where((row8 >> 1) == h, res[168:176, lanes], last)
        sides3.append(jnp.concatenate(tiles, axis=0))
        sides4.append(jnp.concatenate([last, jnp.zeros((8, 128), F32)], axis=0))
    my3 = pl.ds(pl.multiple_of(core * STRIDE3 + (BACK3 + chip) * 32, 32), 32)
    my4 = pl.ds(pl.multiple_of(core * 256 + chip * 16, 16), 16)
    far3[my3, :] = jnp.concatenate(sides3, axis=1).astype(BF16)
    far4[my4, :] = jnp.concatenate(sides4, axis=1).astype(BF16)
    far12[96:160, :] = pool12[0:64, :]

    pl.semaphore_wait(barrier, len(places))

    def remote(src, dst, sends, recvs, slot, place):
        return pltpu.make_async_remote_copy(
            src_ref=src, dst_ref=dst, send_sem=sends.at[slot], recv_sem=recvs.at[slot],
            device_id=place, device_id_type=MESH,
        )

    def later(k):
        return {"seq": lax.rem(me + k, n)}

    def row2(k):
        return 160 + 32 * (3 - k)

    near_copies = [
        remote(pool12.at[128:160], far12.at[row2(k) : row2(k) + 32], near_send, near_recv, k - 1, later(k))
        for k in (1, 2, 3)
    ]
    near_copies.append(remote(pool12.at[32:128], far12.at[0:96], near_send, near_recv, 3, later(1)))
    tail_copy = remote(kvx.at[1024:1280], kvx.at[0:256], near_send, near_recv, 4, later(1))

    def peer_copies(d):
        return (
            remote(far3.at[my3], far3.at[my3], peer_send, peer_recv, d, {"seq": z_peer(d)}),
            remote(far4.at[my4], far4.at[my4], peer_send, peer_recv, 8 + d, {"seq": z_peer(d)}),
        )

    def line_copies(x, slot, place):
        rows3 = pl.ds(pl.multiple_of(core * STRIDE3 + (BACK3 + x * row_chips) * 32, 32), row_chips * 32)
        rows4 = pl.ds(pl.multiple_of(core * 256 + x * 128, 128), row_chips * 16)
        return (
            remote(far3.at[rows3], far3.at[rows3], side_send, side_recv, slot, place),
            remote(far4.at[rows4], far4.at[rows4], side_send, side_recv, slot + 1, place),
        )

    line_sibling = line_copies(x_low, 0, {"seq": sibling})
    line_next = line_copies(0, 2, {"seq": x_next})
    line_last = line_copies(0, 4, {"seq": sibling})

    for d in range(1, row_chips):
        for copy in peer_copies(d):
            copy.start()
    for copy in near_copies:
        copy.start()
    tail_copy.start()

    def w_copy(src, kind, j, rows_of, place):
        rows = pl.ds(pl.multiple_of(rows_of * 128, 128), 128)
        cols = pl.ds(pl.multiple_of(j * 1024, 1024), 1024)
        return remote(src.at[rows, cols], w_in.at[rows, cols], w_send, w_recv, kind * 4 + j, place)

    other = lax.rem(quarter + 2, 4)
    w_across = lambda j: w_copy(w_hbm, 0, j, quarter, across)
    w_sibling = lambda j: w_copy(w_in, 1, j, quarter, {"seq": sibling})
    w_beside = lambda j: w_copy(w_in, 2, j, quarter, {"seq": beside})
    w_last = lambda j: w_copy(w_in, 3, j, other, {"seq": sibling})

    def pass_on(j):
        w_across(j).wait_recv()
        w_sibling(j).start()
        w_beside(j).start()

    def pass_last(j):
        w_beside(j).wait_recv()
        w_last(j).start()

    for j in range(4):
        w_across(j).start()

    qp[...] = dot_nn(pm[176:240, :], qs[...]).astype(BF16)
    fill_interp(wi)
    fill_masks(pick12, pick3, pick4, s0)

    def near(b, h):
        rows = pl.ds(pl.multiple_of(b * 256, 256), 256)
        next_rows = pl.ds(pl.multiple_of(b * 256 + 256, 256), 256)
        lanes = pl.ds(pl.multiple_of(h * 128, 128), 128)
        vlanes = pl.ds(pl.multiple_of(512 + h * 128, 128), 128)
        q = qs[rows, lanes]
        s_prev = dot_nt(q, kvx[rows, lanes])
        s_own = dot_nt(q, kvx[next_rows, lanes])
        s_prev = jnp.where(s0 + b * 256 > 0, s_prev, BIG)
        s_own = jnp.where(iota((256, 256), 1) <= iota((256, 256), 0), s_own, BIG)
        top = jnp.max(jnp.maximum(s_prev, s_own), axis=1, keepdims=True) * SCALE2
        w_prev = jnp.exp2(s_prev * SCALE2 - top)
        w_own = jnp.exp2(s_own * SCALE2 - top)
        total = jnp.sum(w_prev + w_own, axis=1, keepdims=True)
        num[rows, lanes] = dot_nn(w_prev.astype(BF16), kvx[rows, vlanes]) + dot_nn(
            w_own.astype(BF16), kvx[next_rows, vlanes]
        )
        mx[rows, lanes] = jnp.broadcast_to(top, (256, 128))
        den[rows, lanes] = jnp.broadcast_to(total, (256, 128))

    def near_step(i, carry):
        near(i >> 2, i & 3)
        return carry

    lax.fori_loop(4, 12, near_step, 0)
    for d in range(1, row_chips):
        for copy in peer_copies(d):
            copy.wait_recv()
    for copy in line_sibling:
        copy.start()

    @pl.when(x_low == 0)
    def _():
        for copy in line_next:
            copy.start()

    lax.fori_loop(12, 16, near_step, 0)

    @pl.when(x_low == 1)
    def _():
        for copy in line_next:
            copy.wait_recv()
        for copy in line_last:
            copy.start()

    for copy in line_sibling:
        copy.wait_recv()
    for copy in near_copies:
        copy.wait_recv()

    @pl.when(x_low == 1)
    def _():
        for copy in line_last:
            copy.wait_recv()

    windows3 = [pl.ds(pl.multiple_of(c * STRIDE3 + chip * 32, 32), 192) for c in range(2)]
    windows4 = [pl.ds(c * 256, 192) for c in range(2)]

    def two(ref, windows, lanes):
        return jnp.concatenate([ref[w, lanes] for w in windows], axis=0)

    def far(h, carry):
        lanes = pl.ds(pl.multiple_of(h * 128, 128), 128)
        vlanes = pl.ds(pl.multiple_of(512 + h * 128, 128), 128)
        keys, values = slice(0, 128), slice(128, 256)
        pooled = qp[:, lanes]
        parts = [
            (pick12[...] > 0, far12[:, lanes], far12[:, vlanes]),
            (pick3[...] == h, two(far3, windows3, keys), two(far3, windows3, values)),
            (pick4[...] == h, two(far4, windows4, keys), two(far4, windows4, values)),
        ]
        scores = [jnp.where(chosen, dot_nt(pooled, key), BIG) for chosen, key, _ in parts]
        top = functools.reduce(jnp.maximum, [jnp.max(s, axis=1, keepdims=True) for s in scores]) * SCALE2
        weights = [
            jnp.where(chosen, jnp.exp2(s * SCALE2 - top), 0.0) for (chosen, _, _), s in zip(parts, scores)
        ]
        total = sum(jnp.sum(w, axis=1, keepdims=True) for w in weights)
        acc = sum(dot_nn(w.astype(BF16), value) for w, (_, _, value) in zip(weights, parts))
        some = total > 0
        safe = jnp.where(some, total, 1.0)
        lse = jnp.where(some, top + jnp.log(safe) * LOG2E, BIG)
        both = jnp.concatenate([acc / safe, jnp.broadcast_to(lse, (64, 128))], axis=1)
        high = both.astype(BF16)
        rest = both - high.astype(F32)
        middle = rest.astype(BF16)
        low = (rest - middle.astype(F32)).astype(BF16)
        for b in range(4):
            for j, part in enumerate((high, middle, low)):
                fo[h * 4 + b, 16 * j : 16 * (j + 1), :] = part[16 * b : 16 * (b + 1), :]
        return carry

    lax.fori_loop(0, 4, far, 0)

    tail_copy.wait_recv()
    lax.fori_loop(0, 4, near_step, 0)
    pass_on(0)
    pass_on(1)

    y_up, y_down, y_far = lax.rem(y + 1, 4), lax.rem(y + 3, 4), lax.rem(y + 2, 4)
    order = [y_far, y_up, y_down, y]

    def mix(row):
        rows = pl.ds(pl.multiple_of(row, 128), 128)
        b = lax.div(row, 256)
        weights = wi[pl.ds(pl.multiple_of(lax.rem(row, 256), 128), 128), :]

        def one(h, carry):
            lanes = pl.ds(pl.multiple_of(h * 128, 128), 128)
            tok = dot_nn(weights, fo[h * 4 + b])
            tok_out, tok_lse = tok[:, 0:128], tok[:, 128:256]
            near_max = mx[rows, lanes]
            top = jnp.maximum(near_max, tok_lse)
            a = jnp.exp2(near_max - top)
            b_far = jnp.exp2(tok_lse - top)
            mixed = (num[rows, lanes] * a + tok_out * b_far) / (den[rows, lanes] * a + b_far)
            att[rows, lanes] = mixed.astype(BF16)
            return carry

        lax.fori_loop(0, 4, one, 0)

    def give(i):
        target = order[i]
        src = pl.ds(pl.multiple_of((1 - half) * 512 + target * 128, 128), 128)
        dst = pl.ds(pl.multiple_of(target * 128, 128), 128)
        return remote(att.at[src], att_in.at[dst], att_send, att_recv, i, {"head": partner})

    def mix_out(i):
        mix((1 - half) * 512 + order[i] * 128)
        give(i).start()

    def mix_own(i):
        mix(half * 512 + order[i] * 128)

    mix_out(0)
    mix_out(1)
    mix_out(2)
    mix_own(0)
    pass_on(2)
    pass_last(0)
    mix_out(3)
    for i in (1, 2, 3):
        mix_own(i)
    pass_on(3)
    pass_last(1)
    load_w.wait()

    def share(target, chunk):
        own_rows = pl.ds(pl.multiple_of(half * 512 + target * 128, 128), 128)
        in_rows = pl.ds(pl.multiple_of(target * 128, 128), 128)
        cols = pl.ds(pl.multiple_of(chunk * 512, 512), 512)
        return dot_nn(att[own_rows, :], w_own[:, cols]) + dot_nn(att_in[in_rows, :], w_in[:, cols])

    def first_copy(side, j):
        slot = side * 4 + j
        return remote(sb1.at[slot], rb1.at[slot], send1, recv1, slot, {"head": (up, down)[side]})

    def second_copy(side, chunk):
        slot = side * 8 + chunk
        return remote(sb2.at[slot], rb2.at[slot], send2, recv2, slot, {"head": (up, down)[side]})

    def begin(j, carry):
        w_sibling(j).wait_recv()
        w_last(j).wait_recv()
        for side in range(2):
            sb1[side * 4 + j] = share(y_far, 2 * j + side).astype(BF16)
            first_copy(side, j).start()
        return carry

    def direct(j, carry):
        for side in range(2):
            chunk = 2 * j + 1 - side
            sb2[side * 8 + chunk] = share((y_up, y_down)[side], chunk).astype(BF16)
            second_copy(side, chunk).start()
        return carry

    give(0).wait_recv()
    lax.fori_loop(0, 2, begin, 0)
    give(1).wait_recv()
    give(2).wait_recv()
    lax.fori_loop(0, 2, direct, 0)
    pass_last(2)
    pass_last(3)

    def both(j, carry):
        begin(j, carry)
        return direct(j, carry)

    lax.fori_loop(2, 4, both, 0)

    def follow(j, carry):
        for side in range(2):
            chunk = 2 * j + side
            mine = share((y_up, y_down)[side], chunk)
            first_copy(side, j).wait_recv()
            sb2[side * 8 + chunk] = (mine + rb1[side * 4 + j].astype(F32)).astype(BF16)
            second_copy(side, chunk).start()
        return carry

    lax.fori_loop(0, 4, follow, 0)

    give(3).wait_recv()

    def keep(chunk, carry):
        own[chunk] = share(y, chunk)
        return carry

    lax.fori_loop(0, 8, keep, 0)

    def finish(chunk, carry):
        for side in range(2):
            second_copy(side, chunk).wait_recv()
        total = own[chunk] + rb2[chunk].astype(F32) + rb2[8 + chunk].astype(F32)
        out[:, pl.ds(pl.multiple_of(chunk * 512, 512), 512)] = total.astype(BF16)
        return carry

    lax.fori_loop(0, 8, finish, 0)

    for d in range(1, row_chips):
        for copy in peer_copies(d):
            copy.wait_send()
    for copy in near_copies + [tail_copy] + list(line_sibling):
        copy.wait_send()

    @pl.when(x_low == 0)
    def _():
        for copy in line_next:
            copy.wait_send()

    @pl.when(x_low == 1)
    def _():
        for copy in line_last:
            copy.wait_send()

    for j in range(4):
        w_across(j).wait_send()
        w_sibling(j).wait_send()
        w_beside(j).wait_send()
        w_last(j).wait_send()
        for side in range(2):
            first_copy(side, j).wait_send()
            second_copy(side, j).wait_send()
            second_copy(side, 4 + j).wait_send()
    for i in range(4):
        give(i).wait_send()


def layer(n, q, k, v, w):
    hbm_spec = pl.BlockSpec(memory_space=pltpu.HBM)
    vm = pltpu.VMEM
    return pl.pallas_call(
        functools.partial(kernel, n),
        out_shape=jax.ShapeDtypeStruct((128, 4096), BF16),
        in_specs=[hbm_spec] * 4,
        out_specs=pl.BlockSpec(memory_space=pltpu.VMEM),
        scratch_shapes=[
            vm((1280, 1024), BF16),
            vm((1024, 512), BF16),
            vm((240, 1024), BF16),
            vm((256, 48), BF16),
            vm((176, 1024), F32),
            vm((160, 1024), BF16),
            vm((64, 512), BF16),
            vm((256, 1024), BF16),
            vm((2 * STRIDE3, 256), BF16),
            vm((512, 256), BF16),
            vm((64, 256), jnp.int32),
            vm((64, 384), jnp.int32),
            vm((64, 384), jnp.int32),
            vm((16, 48, 256), BF16),
            vm((1024, 512), F32),
            vm((1024, 512), F32),
            vm((1024, 512), F32),
            vm((1024, 512), BF16),
            vm((512, 512), BF16),
            vm((512, 4096), BF16),
            vm((512, 4096), BF16),
            vm((8, 128, 512), BF16),
            vm((8, 128, 512), BF16),
            vm((16, 128, 512), BF16),
            vm((16, 128, 512), BF16),
            vm((8, 128, 512), F32),
            pltpu.SemaphoreType.DMA((4,)),
        ]
        + [pltpu.SemaphoreType.DMA((count,)) for count in (5, 5, 16, 16, 6, 6, 4, 4, 16, 16, 8, 8, 16, 16)],
        compiler_params=pltpu.CompilerParams(
            collective_id=0, has_side_effects=True, vmem_limit_bytes=56 * 1024 * 1024
        ),
        cost_estimate=pl.CostEstimate(flops=6 * 10**9, bytes_accessed=8 * 2**20, transcendentals=2 * 10**6),
    )(q, k, v, w)


def solution(mesh):
    n = mesh.shape["seq"]

    def body(queries, key_tokens, value_tokens, out_weight):
        return layer(n, queries, key_tokens, value_tokens, out_weight)

    in_specs = (P("seq", "head"), P("seq", "head"), P("seq", "head"), P("head", None))
    out_specs = P(("seq", "head"), None)
    return jax.shard_map(body, mesh=mesh, in_specs=in_specs, out_specs=out_specs, check_vma=False)
```

```python
import functools
import math

import jax
import jax.numpy as jnp
from jax import lax
from jax.experimental import pallas as pl
from jax.experimental.pallas import tpu as pltpu
from jax.sharding import PartitionSpec as P

MESH = pl.DeviceIdType.MESH
HD = 128
BLK = 256
QG = 16
LOG2E = 1.4426950408889634
SCALE2 = LOG2E / math.sqrt(HD)
BIG = -1e30
F32 = jnp.float32
BF16 = jnp.bfloat16

BACK3 = 6
STRIDE3 = 704


def iota(shape, dim):
    return lax.broadcasted_iota(jnp.int32, shape, dim)


def dot_nt(a, b):
    return lax.dot_general(a, b, (((1,), (1,)), ((), ())), preferred_element_type=F32)


def dot_nn(a, b):
    return jnp.dot(a, b, preferred_element_type=F32)


def fill_pool_matrix(pm):
    def piece(rows, shift, weight):
        hit = (iota((rows, 1024), 1) >> shift) == iota((rows, 1024), 0)
        return jnp.where(hit, weight, 0.0).astype(BF16)

    pm[0:128, :] = piece(128, 3, 1.0 / 8)
    pm[128:160, :] = piece(32, 5, 1.0 / 32)
    row, col = iota((16, 1024), 0), iota((16, 1024), 1)
    third = jnp.where((col >> 7) == row, 1.0 / 128, 0.0)
    fourth = jnp.where((col >> 9) == (row & 1), 1.0 / 512, 0.0)
    pm[160:176, :] = jnp.where(row < 8, third, fourth).astype(BF16)
    pm[176:240, :] = piece(64, 4, 1.0 / 16)


def fill_interp(wi):
    row, col = iota((BLK, 48), 0), iota((BLK, 48), 1)
    numer = 2 * row - (QG - 1)
    low = jnp.clip(numer >> 5, 0, BLK // QG - 2)
    frac = jnp.clip((numer - low * 32).astype(F32) * (1.0 / 32), 0.0, 1.0)
    group = col & 15
    value = jnp.where(group == low, 1.0 - frac, 0.0) + jnp.where(group == low + 1, frac, 0.0)
    wi[...] = value.astype(BF16)


def bounds(start):
    first = jnp.maximum(start - 256, 0)
    second = jnp.maximum(((first - 512) >> 5) << 5, 0)
    third = jnp.maximum(((second - 2048) >> 7) << 7, 0)
    fourth = jnp.maximum(((third - 8192) >> 9) << 9, 0)
    return first, second, third, fourth


def fill_masks(pick12, pick3, pick4, s0):
    shape = (64, 256)
    first, second, third, fourth = bounds(s0 + 256 * (iota(shape, 0) >> 4))
    col = iota(shape, 1)
    is_first = col < 160
    token = jnp.where(is_first, s0 - 768 + 8 * col, s0 - 3072 + 32 * (col - 160))
    size = jnp.where(is_first, 8, 32)
    lower = jnp.where(is_first, second, third)
    upper = jnp.where(is_first, first, second)
    pick12[...] = jnp.where((token >= lower) & (token + size <= upper), 1, 0)
    shape = (64, 384)
    first, second, third, fourth = bounds(s0 + 256 * (iota(shape, 0) >> 4))
    col = iota(shape, 1)
    core = jnp.where(col < 192, 0, 1)
    rest = col - 192 * core
    token = ((s0 >> 11) - BACK3 + (rest >> 5)) * 2048 + core * 1024 + (rest & 7) * 128
    chosen = (token >= fourth) & (token + 128 <= third)
    pick3[...] = jnp.where(chosen, (rest & 31) >> 3, -1)
    token = (rest >> 4) * 2048 + core * 1024 + (rest & 1) * 512
    chosen = (token >= 0) & (token + 512 <= fourth)
    pick4[...] = jnp.where(chosen, (rest & 15) >> 1, -1)


def kernel(
    n, q_hbm, k_hbm, v_hbm, w_hbm, result,
    kvx, qs, pm, wi, res, pool12, qp, far12, far3, far4, pick12, pick3, pick4, fo, num, mx, den,
    att, att_in, w_own, w_in, sb1, rb1, sb2, rb2, own, out,
    load_sem, near_send, near_recv, peer_send, peer_recv, side_send, side_recv,
    att_send, att_recv, w_send, w_recv, send1, recv1, send2, recv2, out_sem,
):
    me = lax.axis_index("seq")
    head = lax.axis_index("head")
    s0 = me * 1024
    chips = n // 2
    row_chips = chips // 2
    core = lax.rem(me, 2)
    chip = lax.div(me, 2)
    x_low = lax.div(chip, row_chips)
    z = lax.rem(chip, row_chips)
    half = lax.div(head, 4)
    y = lax.rem(head, 4)
    partner = lax.rem(head + 4, 8)
    up = half * 4 + lax.rem(y + 1, 4)
    down = half * 4 + lax.rem(y + 3, 4)
    x_next = lax.rem(me + chips, n)
    across = {"seq": x_next, "head": partner}
    side_x = x_low * 2 + core
    side_z = lax.rem(me, 4)
    beside_z = me + 2 - 4 * lax.div(side_z, 2)
    sibling = me + 1 - 2 * core

    def z_peer(d):
        return x_low * chips + lax.rem(z + d, row_chips) * 2 + core

    barrier = pltpu.get_barrier_semaphore()
    for c in range(2):
        far3[c * STRIDE3 : c * STRIDE3 + BACK3 * 32, :] = jnp.zeros((BACK3 * 32, 256), BF16)
        far4[c * 256 + 128 : c * 256 + 256, :] = jnp.zeros((128, 256), BF16)
    places = [{"seq": z_peer(d)} for d in range(1, row_chips)]
    places += [{"seq": lax.rem(me + n - k, n)} for k in (1, 2, 3 - 2 * core)]
    places += [{"seq": sibling}, {"seq": x_next}, {"head": partner}, {"head": up}, {"head": down}, across]
    for place in places:
        pl.semaphore_signal(barrier, inc=1, device_id=place, device_id_type=MESH)

    load_k = pltpu.make_async_copy(k_hbm, kvx.at[256:1280, 0:512], load_sem.at[0])
    load_v = pltpu.make_async_copy(v_hbm, kvx.at[256:1280, 512:1024], load_sem.at[1])
    load_q = pltpu.make_async_copy(q_hbm, qs, load_sem.at[2])
    load_w = pltpu.make_async_copy(w_hbm, w_own, load_sem.at[3])
    load_k.start()
    load_v.start()
    load_q.start()

    def remote(src, dst, sends, recvs, slot, place):
        return pltpu.make_async_remote_copy(
            src_ref=src, dst_ref=dst, send_sem=sends.at[slot], recv_sem=recvs.at[slot],
            device_id=place, device_id_type=MESH,
        )

    def later(k):
        return {"seq": lax.rem(me + k, n)}

    def w_copy(src, kind, j, rows_of, place):
        rows = pl.ds(pl.multiple_of(rows_of * 128, 128), 128)
        cols = pl.ds(pl.multiple_of(j * 1024, 1024), 1024)
        return remote(src.at[rows, cols], w_in.at[rows, cols], w_send, w_recv, kind * 4 + j, place)

    def place_of(j):
        if j < 2:
            return side_x, lax.rem(side_x + 2, 4), x_next
        return side_z, side_z, beside_z

    def w_across(j):
        return w_copy(w_hbm, 0, j, place_of(j)[1], across)

    def w_sibling(j):
        return w_copy(w_in, 1, j, place_of(j)[0], {"seq": sibling})

    def w_beside(j):
        return w_copy(w_in, 2, j, place_of(j)[0], {"seq": place_of(j)[2]})

    def w_last(j):
        return w_copy(w_in, 3, j, lax.rem(place_of(j)[0] + 2, 4), {"seq": sibling})

    def pass_on(j):
        w_across(j).wait_recv()
        w_sibling(j).start()
        w_beside(j).start()

    def pass_last(j):
        w_beside(j).wait_recv()
        w_last(j).start()

    tail_copies = [
        remote(ref.at[768:1024], kvx.at[0:256, i * 512 : i * 512 + 512], near_send, near_recv, 4 + i, later(1))
        for i, ref in enumerate((k_hbm, v_hbm))
    ]

    fill_pool_matrix(pm)
    pl.semaphore_wait(barrier, len(places))
    for copy in tail_copies:
        copy.start()
    w_across(0).start()

    def pool(c, carry):
        cols = pl.ds(pl.multiple_of(c * 256, 256), 256)
        res[:, cols] = dot_nn(pm[0:176, :], kvx[256:1280, cols])
        return carry

    load_k.wait()
    lax.fori_loop(0, 2, pool, 0)
    load_v.wait()
    lax.fori_loop(2, 4, pool, 0)
    pool12[...] = res[0:160, :].astype(BF16)
    row8 = iota((8, 128), 0)
    sides3, sides4 = [], []
    for side in range(2):
        tiles = [res[160:168, side * 512 + h * 128 : side * 512 + (h + 1) * 128] for h in range(4)]
        last = jnp.zeros((8, 128), F32)
        for h in range(4):
            lanes = slice(side * 512 + h * 128, side * 512 + (h + 1) * 128)
            last = jnp.where((row8 >> 1) == h, res[168:176, lanes], last)
        sides3.append(jnp.concatenate(tiles, axis=0))
        sides4.append(jnp.concatenate([last, jnp.zeros((8, 128), F32)], axis=0))
    my3 = pl.ds(pl.multiple_of(core * STRIDE3 + (BACK3 + chip) * 32, 32), 32)
    my4 = pl.ds(pl.multiple_of(core * 256 + chip * 16, 16), 16)
    far3[my3, :] = jnp.concatenate(sides3, axis=1).astype(BF16)
    far4[my4, :] = jnp.concatenate(sides4, axis=1).astype(BF16)
    far12[96:160, :] = pool12[0:64, :]

    def rows2(row):
        return far12.at[pl.ds(pl.multiple_of(row, 32), 32)]

    own2 = pool12.at[128:160]
    second_far = 1 + 2 * core
    near_copies = [
        remote(own2, rows2(192), near_send, near_recv, 0, later(2)),
        remote(own2, rows2(224 - 64 * core), near_send, near_recv, 1, later(second_far)),
        remote(pool12.at[32:128], far12.at[0:96], near_send, near_recv, 2, later(1)),
    ]
    pass2 = remote(rows2(192), rows2(160 + 64 * core), near_send, near_recv, 3, {"seq": sibling})
    def peer_copies(d):
        return (
            remote(far3.at[my3], far3.at[my3], peer_send, peer_recv, d, {"seq": z_peer(d)}),
            remote(far4.at[my4], far4.at[my4], peer_send, peer_recv, 8 + d, {"seq": z_peer(d)}),
        )

    def line_copies(x, slot, place):
        rows3 = pl.ds(pl.multiple_of(core * STRIDE3 + (BACK3 + x * row_chips) * 32, 32), row_chips * 32)
        rows4 = pl.ds(pl.multiple_of(core * 256 + x * 128, 128), row_chips * 16)
        return (
            remote(far3.at[rows3], far3.at[rows3], side_send, side_recv, slot, place),
            remote(far4.at[rows4], far4.at[rows4], side_send, side_recv, slot + 1, place),
        )

    line_sibling = line_copies(x_low, 0, {"seq": sibling})
    line_next = line_copies(0, 2, {"seq": x_next})
    line_last = line_copies(0, 4, {"seq": sibling})

    for d in range(1, row_chips):
        for copy in peer_copies(d):
            copy.start()
    for copy in near_copies:
        copy.start()
    load_q.wait()
    load_w.start()

    qp[...] = dot_nn(pm[176:240, :], qs[...]).astype(BF16)
    fill_interp(wi)
    fill_masks(pick12, pick3, pick4, s0)

    def near(b, h):
        rows = pl.ds(pl.multiple_of(b * 256, 256), 256)
        next_rows = pl.ds(pl.multiple_of(b * 256 + 256, 256), 256)
        lanes = pl.ds(pl.multiple_of(h * 128, 128), 128)
        vlanes = pl.ds(pl.multiple_of(512 + h * 128, 128), 128)
        q = qs[rows, lanes]
        s_prev = dot_nt(q, kvx[rows, lanes])
        s_own = dot_nt(q, kvx[next_rows, lanes])
        s_prev = jnp.where(s0 + b * 256 > 0, s_prev, BIG)
        s_own = jnp.where(iota((256, 256), 1) <= iota((256, 256), 0), s_own, BIG)
        top = jnp.max(jnp.maximum(s_prev, s_own), axis=1, keepdims=True) * SCALE2
        w_prev = jnp.exp2(s_prev * SCALE2 - top)
        w_own = jnp.exp2(s_own * SCALE2 - top)
        ones = jnp.ones((256, 128), BF16)
        acc = dot_nn(w_prev.astype(BF16), jnp.concatenate([kvx[rows, vlanes], ones], axis=1))
        acc += dot_nn(w_own.astype(BF16), jnp.concatenate([kvx[next_rows, vlanes], ones], axis=1))
        num[rows, lanes] = acc[:, 0:128]
        den[rows, lanes] = acc[:, 128:256]
        mx[rows, lanes] = jnp.broadcast_to(top, (256, 128))

    def near_step(i, carry):
        near(i >> 1, (i & 1) * 2)
        near(i >> 1, (i & 1) * 2 + 1)
        return carry

    w_across(1).start()
    lax.fori_loop(2, 5, near_step, 0)
    pass_on(0)
    lax.fori_loop(5, 6, near_step, 0)
    for d in range(1, row_chips):
        for copy in peer_copies(d):
            copy.wait_recv()
    for copy in line_sibling:
        copy.start()

    @pl.when(x_low == 0)
    def _():
        for copy in line_next:
            copy.start()

    near_copies[0].wait_recv()
    pass2.start()
    w_across(2).start()
    lax.fori_loop(6, 8, near_step, 0)
    for copy in tail_copies:
        copy.wait_recv()
    lax.fori_loop(0, 2, near_step, 0)
    pass_on(1)
    w_across(3).start()

    @pl.when(x_low == 1)
    def _():
        for copy in line_next:
            copy.wait_recv()
        for copy in line_last:
            copy.start()

    pass_last(0)
    for copy in line_sibling:
        copy.wait_recv()
    for copy in near_copies[1:] + [pass2]:
        copy.wait_recv()

    @pl.when(x_low == 1)
    def _():
        for copy in line_last:
            copy.wait_recv()

    windows3 = [pl.ds(pl.multiple_of(c * STRIDE3 + chip * 32, 32), 192) for c in range(2)]
    windows4 = [pl.ds(c * 256, 192) for c in range(2)]

    def two(ref, windows, lanes):
        return jnp.concatenate([ref[w, lanes] for w in windows], axis=0)

    def far(h):
        lanes = slice(h * 128, h * 128 + 128)
        vlanes = slice(512 + h * 128, 640 + h * 128)
        keys, values = slice(0, 128), slice(128, 256)
        pooled = qp[:, lanes]
        parts = [
            (pick12[...] > 0, far12[:, lanes], far12[:, vlanes]),
            (pick3[...] == h, two(far3, windows3, keys), two(far3, windows3, values)),
            (pick4[...] == h, two(far4, windows4, keys), two(far4, windows4, values)),
        ]
        scores = [jnp.where(chosen, dot_nt(pooled, key), BIG) for chosen, key, _ in parts]
        top = functools.reduce(jnp.maximum, [jnp.max(s, axis=1, keepdims=True) for s in scores]) * SCALE2
        weights = [
            jnp.where(chosen, jnp.exp2(s * SCALE2 - top), 0.0) for (chosen, _, _), s in zip(parts, scores)
        ]
        total = sum(jnp.sum(w, axis=1, keepdims=True) for w in weights)
        acc = sum(dot_nn(w.astype(BF16), value) for w, (_, _, value) in zip(weights, parts))
        some = total > 0
        safe = jnp.where(some, total, 1.0)
        lse = jnp.where(some, top + jnp.log(safe) * LOG2E, BIG)
        both = jnp.concatenate([acc / safe, jnp.broadcast_to(lse, (64, 128))], axis=1)
        high = both.astype(BF16)
        rest = both - high.astype(F32)
        middle = rest.astype(BF16)
        low = (rest - middle.astype(F32)).astype(BF16)
        for b in range(4):
            for j, part in enumerate((high, middle, low)):
                fo[h * 4 + b, 16 * j : 16 * (j + 1), :] = part[16 * b : 16 * (b + 1), :]

    for h in range(4):
        far(h)
    pass_on(2)
    pass_last(1)

    y_up, y_down, y_far = lax.rem(y + 1, 4), lax.rem(y + 3, 4), lax.rem(y + 2, 4)

    def mix(row):
        rows = pl.ds(pl.multiple_of(row, 128), 128)
        b = lax.div(row, 256)
        weights = wi[pl.ds(pl.multiple_of(lax.rem(row, 256), 128), 128), :]

        for h in range(4):
            lanes = slice(h * 128, h * 128 + 128)
            tok = dot_nn(weights, fo[h * 4 + b])
            tok_out, tok_lse = tok[:, 0:128], tok[:, 128:256]
            near_max = mx[rows, lanes]
            top = jnp.maximum(near_max, tok_lse)
            a = jnp.exp2(near_max - top)
            b_far = jnp.exp2(tok_lse - top)
            mixed = (num[rows, lanes] * a + tok_out * b_far) / (den[rows, lanes] * a + b_far)
            att[rows, lanes] = mixed.astype(BF16)

    def give(target):
        src = pl.ds(pl.multiple_of((1 - half) * 512 + target * 128, 128), 128)
        dst = pl.ds(pl.multiple_of(target * 128, 128), 128)
        return remote(att.at[src], att_in.at[dst], att_send, att_recv, target, {"head": partner})

    def mix_out(target):
        mix((1 - half) * 512 + target * 128)

    def mix_own(target):
        mix(half * 512 + target * 128)

    mix_out(y_far)
    give(y_far).start()
    mix_own(y_far)
    mix_out(y_up)
    give(y_up).start()
    mix_out(y_down)
    mix_own(y_up)
    mix_own(y_down)
    mix_out(y)
    mix_own(y)
    load_w.wait()

    def share(target, chunk):
        own_rows = pl.ds(pl.multiple_of(half * 512 + target * 128, 128), 128)
        in_rows = pl.ds(pl.multiple_of(target * 128, 128), 128)
        cols = pl.ds(pl.multiple_of(chunk * 512, 512), 512)
        return dot_nn(att[own_rows, :], w_own[:, cols]) + dot_nn(att_in[in_rows, :], w_in[:, cols])

    def first_copy(side, j):
        slot = side * 4 + j
        return remote(sb1.at[slot], rb1.at[slot], send1, recv1, slot, {"head": (up, down)[side]})

    def second_copy(side, chunk):
        slot = side * 8 + chunk
        return remote(sb2.at[slot], rb2.at[slot], send2, recv2, slot, {"head": (up, down)[side]})

    def w_ready(j):
        w_sibling(j).wait_recv()
        w_last(j).wait_recv()

    def begin(j, carry):
        for side in range(2):
            sb1[side * 4 + j] = share(y_far, 2 * j + side).astype(BF16)
            first_copy(side, j).start()
        return carry

    def direct(side, j):
        chunk = 2 * j + 1 - side
        sb2[side * 8 + chunk] = share((y_up, y_down)[side], chunk).astype(BF16)
        second_copy(side, chunk).start()

    def direct_up(j, carry):
        direct(0, j)
        return carry

    def direct_down(j, carry):
        direct(1, j)
        return carry

    def both(j, carry):
        begin(j, carry)
        direct(0, j)
        direct(1, j)
        return carry

    give(y_far).wait_send()
    give(y_down).start()
    give(y_far).wait_recv()
    w_ready(0)
    lax.fori_loop(0, 1, begin, 0)
    pass_on(3)
    w_ready(1)
    lax.fori_loop(1, 2, begin, 0)
    give(y_up).wait_send()
    give(y).start()
    give(y_up).wait_recv()
    lax.fori_loop(0, 2, direct_up, 0)
    give(y_down).wait_send()
    give(y_down).wait_recv()
    lax.fori_loop(0, 2, direct_down, 0)
    pass_last(2)
    w_ready(2)
    lax.fori_loop(2, 3, both, 0)
    pass_last(3)
    w_ready(3)
    lax.fori_loop(3, 4, both, 0)

    def follow(j, carry):
        for side in range(2):
            chunk = 2 * j + side
            mine = share((y_up, y_down)[side], chunk)
            first_copy(side, j).wait_recv()
            sb2[side * 8 + chunk] = (mine + rb1[side * 4 + j].astype(F32)).astype(BF16)
            second_copy(side, chunk).start()
        return carry

    lax.fori_loop(0, 4, follow, 0)

    give(y).wait_recv()

    def keep(chunk, carry):
        own[chunk] = share(y, chunk)
        return carry

    lax.fori_loop(0, 8, keep, 0)

    def store(chunk):
        cols = pl.ds(pl.multiple_of(chunk * 512, 512), 512)
        return pltpu.make_async_copy(out.at[:, cols], result.at[:, cols], out_sem.at[chunk])

    def finish(chunk, carry):
        for side in range(2):
            second_copy(side, chunk).wait_recv()
        total = own[chunk] + rb2[chunk].astype(F32) + rb2[8 + chunk].astype(F32)
        out[:, pl.ds(pl.multiple_of(chunk * 512, 512), 512)] = total.astype(BF16)
        store(chunk).start()
        return carry

    lax.fori_loop(0, 8, finish, 0)

    for d in range(1, row_chips):
        for copy in peer_copies(d):
            copy.wait_send()
    for copy in near_copies + [pass2] + tail_copies + list(line_sibling):
        copy.wait_send()

    @pl.when(x_low == 0)
    def _():
        for copy in line_next:
            copy.wait_send()

    @pl.when(x_low == 1)
    def _():
        for copy in line_last:
            copy.wait_send()

    for j in range(4):
        w_across(j).wait_send()
        w_sibling(j).wait_send()
        w_beside(j).wait_send()
        w_last(j).wait_send()
        for side in range(2):
            first_copy(side, j).wait_send()
            second_copy(side, j).wait_send()
            second_copy(side, 4 + j).wait_send()
    for chunk in range(8):
        store(chunk).wait()
    give(y).wait_send()


def layer(n, q, k, v, w):
    hbm_spec = pl.BlockSpec(memory_space=pltpu.HBM)
    vm = pltpu.VMEM
    return pl.pallas_call(
        functools.partial(kernel, n),
        out_shape=jax.ShapeDtypeStruct((128, 4096), BF16),
        in_specs=[hbm_spec] * 4,
        out_specs=pl.BlockSpec(memory_space=pl.ANY),
        scratch_shapes=[
            vm((1280, 1024), BF16),
            vm((1024, 512), BF16),
            vm((240, 1024), BF16),
            vm((256, 48), BF16),
            vm((176, 1024), F32),
            vm((160, 1024), BF16),
            vm((64, 512), BF16),
            vm((256, 1024), BF16),
            vm((2 * STRIDE3, 256), BF16),
            vm((512, 256), BF16),
            vm((64, 256), jnp.int32),
            vm((64, 384), jnp.int32),
            vm((64, 384), jnp.int32),
            vm((16, 48, 256), BF16),
            vm((1024, 512), F32),
            vm((1024, 512), F32),
            vm((1024, 512), F32),
            vm((1024, 512), BF16),
            vm((512, 512), BF16),
            vm((512, 4096), BF16),
            vm((512, 4096), BF16),
            vm((8, 128, 512), BF16),
            vm((8, 128, 512), BF16),
            vm((16, 128, 512), BF16),
            vm((16, 128, 512), BF16),
            vm((8, 128, 512), F32),
            vm((128, 4096), BF16),
            pltpu.SemaphoreType.DMA((4,)),
        ]
        + [pltpu.SemaphoreType.DMA((count,)) for count in (6, 6, 16, 16, 6, 6, 4, 4, 16, 16, 8, 8, 16, 16, 8)],
        compiler_params=pltpu.CompilerParams(
            collective_id=0, has_side_effects=True, vmem_limit_bytes=52 * 1024 * 1024
        ),
        cost_estimate=pl.CostEstimate(flops=6 * 10**9, bytes_accessed=8 * 2**20, transcendentals=2 * 10**6),
    )(q, k, v, w)


def solution(mesh):
    n = mesh.shape["seq"]

    def body(queries, key_tokens, value_tokens, out_weight):
        return layer(n, queries, key_tokens, value_tokens, out_weight)

    in_specs = (P("seq", "head"), P("seq", "head"), P("seq", "head"), P("head", None))
    out_specs = P(("seq", "head"), None)
    return jax.shard_map(body, mesh=mesh, in_specs=in_specs, out_specs=out_specs, check_vma=False)
```

```python
import functools
import math

import jax
import jax.numpy as jnp
from jax import lax
from jax.experimental import pallas as pl
from jax.experimental.pallas import tpu as pltpu
from jax.sharding import PartitionSpec as P

MESH = pl.DeviceIdType.MESH
HD = 128
BLK = 256
QG = 16
LOG2E = 1.4426950408889634
SCALE2 = LOG2E / math.sqrt(HD)
BIG = -1e30
F32 = jnp.float32
BF16 = jnp.bfloat16

BACK3 = 6
STRIDE3 = 704


def iota(shape, dim):
    return lax.broadcasted_iota(jnp.int32, shape, dim)


def dot_nt(a, b):
    return lax.dot_general(a, b, (((1,), (1,)), ((), ())), preferred_element_type=F32)


def dot_nn(a, b):
    return jnp.dot(a, b, preferred_element_type=F32)


def fill_pool_matrix(pm):
    def piece(rows, shift, weight):
        hit = (iota((rows, 1024), 1) >> shift) == iota((rows, 1024), 0)
        return jnp.where(hit, weight, 0.0).astype(BF16)

    pm[0:128, :] = piece(128, 3, 1.0 / 8)
    pm[128:160, :] = piece(32, 5, 1.0 / 32)
    row, col = iota((16, 1024), 0), iota((16, 1024), 1)
    third = jnp.where((col >> 7) == row, 1.0 / 128, 0.0)
    fourth = jnp.where((col >> 9) == (row & 1), 1.0 / 512, 0.0)
    pm[160:176, :] = jnp.where(row < 8, third, fourth).astype(BF16)
    pm[176:240, :] = piece(64, 4, 1.0 / 16)


def fill_interp(wi):
    row, col = iota((BLK, 48), 0), iota((BLK, 48), 1)
    numer = 2 * row - (QG - 1)
    low = jnp.clip(numer >> 5, 0, BLK // QG - 2)
    frac = jnp.clip((numer - low * 32).astype(F32) * (1.0 / 32), 0.0, 1.0)
    group = col & 15
    value = jnp.where(group == low, 1.0 - frac, 0.0) + jnp.where(group == low + 1, frac, 0.0)
    wi[...] = value.astype(BF16)


def bounds(start):
    first = jnp.maximum(start - 256, 0)
    second = jnp.maximum(((first - 512) >> 5) << 5, 0)
    third = jnp.maximum(((second - 2048) >> 7) << 7, 0)
    fourth = jnp.maximum(((third - 8192) >> 9) << 9, 0)
    return first, second, third, fourth


def fill_masks(pick12, pick3, pick4, s0):
    shape = (64, 256)
    first, second, third, fourth = bounds(s0 + 256 * (iota(shape, 0) >> 4))
    col = iota(shape, 1)
    is_first = col < 160
    token = jnp.where(is_first, s0 - 768 + 8 * col, s0 - 3072 + 32 * (col - 160))
    size = jnp.where(is_first, 8, 32)
    lower = jnp.where(is_first, second, third)
    upper = jnp.where(is_first, first, second)
    pick12[...] = jnp.where((token >= lower) & (token + size <= upper), 1, 0)
    shape = (64, 384)
    first, second, third, fourth = bounds(s0 + 256 * (iota(shape, 0) >> 4))
    col = iota(shape, 1)
    core = jnp.where(col < 192, 0, 1)
    rest = col - 192 * core
    token = ((s0 >> 11) - BACK3 + (rest >> 5)) * 2048 + core * 1024 + (rest & 7) * 128
    chosen = (token >= fourth) & (token + 128 <= third)
    pick3[...] = jnp.where(chosen, (rest & 31) >> 3, -1)
    token = (rest >> 4) * 2048 + core * 1024 + (rest & 1) * 512
    chosen = (token >= 0) & (token + 512 <= fourth)
    pick4[...] = jnp.where(chosen, (rest & 15) >> 1, -1)


def kernel(
    n, q_hbm, k_hbm, v_hbm, w_hbm, result,
    kvx, qs, pm, wi, res, pool12, qp, far12, far3, far4, pick12, pick3, pick4, fo, num, mx, den,
    att, att_in, w_own, w_in, sb1, rb1, sb2, rb2, own, out,
    load_sem, near_send, near_recv, peer_send, peer_recv, side_send, side_recv,
    att_send, att_recv, w_send, w_recv, send1, recv1, send2, recv2, out_sem,
):
    me = lax.axis_index("seq")
    head = lax.axis_index("head")
    s0 = me * 1024
    chips = n // 2
    row_chips = chips // 2
    core = lax.rem(me, 2)
    chip = lax.div(me, 2)
    x_low = lax.div(chip, row_chips)
    z = lax.rem(chip, row_chips)
    half = lax.div(head, 4)
    y = lax.rem(head, 4)
    partner = lax.rem(head + 4, 8)
    up = half * 4 + lax.rem(y + 1, 4)
    down = half * 4 + lax.rem(y + 3, 4)
    x_next = lax.rem(me + chips, n)
    across = {"seq": x_next, "head": partner}
    side_x = x_low * 2 + core
    side_z = lax.rem(me, 4)
    beside_z = me + 2 - 4 * lax.div(side_z, 2)
    sibling = me + 1 - 2 * core

    def z_peer(d):
        return x_low * chips + lax.rem(z + d, row_chips) * 2 + core

    barrier = pltpu.get_barrier_semaphore()
    for c in range(2):
        far3[c * STRIDE3 : c * STRIDE3 + BACK3 * 32, :] = jnp.zeros((BACK3 * 32, 256), BF16)
        far4[c * 256 + 128 : c * 256 + 256, :] = jnp.zeros((128, 256), BF16)
    places = [{"seq": z_peer(d)} for d in range(1, row_chips)]
    places += [{"seq": lax.rem(me + n - k, n)} for k in (1, 2, 3 - 2 * core)]
    places += [{"seq": sibling}, {"seq": x_next}, {"head": partner}, {"head": up}, {"head": down}, across]
    for place in places:
        pl.semaphore_signal(barrier, inc=1, device_id=place, device_id_type=MESH)

    load_k = pltpu.make_async_copy(k_hbm, kvx.at[256:1280, 0:512], load_sem.at[0])
    load_v = pltpu.make_async_copy(v_hbm, kvx.at[256:1280, 512:1024], load_sem.at[1])
    load_q = pltpu.make_async_copy(q_hbm, qs, load_sem.at[2])
    load_w = pltpu.make_async_copy(w_hbm, w_own, load_sem.at[3])
    load_k.start()
    load_v.start()
    load_q.start()

    def remote(src, dst, sends, recvs, slot, place):
        return pltpu.make_async_remote_copy(
            src_ref=src, dst_ref=dst, send_sem=sends.at[slot], recv_sem=recvs.at[slot],
            device_id=place, device_id_type=MESH,
        )

    def later(k):
        return {"seq": lax.rem(me + k, n)}

    def w_copy(src, kind, j, rows_of, place):
        rows = pl.ds(pl.multiple_of(rows_of * 128, 128), 128)
        cols = pl.ds(pl.multiple_of(j * 1024, 1024), 1024)
        return remote(src.at[rows, cols], w_in.at[rows, cols], w_send, w_recv, kind * 4 + j, place)

    def place_of(j):
        return side_z, side_z, beside_z

    def w_across(j):
        return w_copy(w_hbm, 0, j, place_of(j)[1], across)

    def w_sibling(j):
        return w_copy(w_in, 1, j, place_of(j)[0], {"seq": sibling})

    def w_beside(j):
        return w_copy(w_in, 2, j, place_of(j)[0], {"seq": place_of(j)[2]})

    def w_last(j):
        return w_copy(w_in, 3, j, lax.rem(place_of(j)[0] + 2, 4), {"seq": sibling})

    def pass_on(j):
        w_across(j).wait_recv()
        w_sibling(j).start()
        w_beside(j).start()

    def pass_last(j):
        w_beside(j).wait_recv()
        w_last(j).start()

    tail_copies = [
        remote(ref.at[768:1024], kvx.at[0:256, i * 512 : i * 512 + 512], near_send, near_recv, 4 + i, later(1))
        for i, ref in enumerate((k_hbm, v_hbm))
    ]

    fill_pool_matrix(pm)
    pl.semaphore_wait(barrier, len(places))
    for copy in tail_copies:
        copy.start()
    w_across(0).start()

    def pool(c, carry):
        cols = pl.ds(pl.multiple_of(c * 256, 256), 256)
        res[:, cols] = dot_nn(pm[0:176, :], kvx[256:1280, cols])
        return carry

    load_k.wait()
    lax.fori_loop(0, 2, pool, 0)
    load_v.wait()
    lax.fori_loop(2, 4, pool, 0)
    pool12[...] = res[0:160, :].astype(BF16)
    row8 = iota((8, 128), 0)
    sides3, sides4 = [], []
    for side in range(2):
        tiles = [res[160:168, side * 512 + h * 128 : side * 512 + (h + 1) * 128] for h in range(4)]
        last = jnp.zeros((8, 128), F32)
        for h in range(4):
            lanes = slice(side * 512 + h * 128, side * 512 + (h + 1) * 128)
            last = jnp.where((row8 >> 1) == h, res[168:176, lanes], last)
        sides3.append(jnp.concatenate(tiles, axis=0))
        sides4.append(jnp.concatenate([last, jnp.zeros((8, 128), F32)], axis=0))
    my3 = pl.ds(pl.multiple_of(core * STRIDE3 + (BACK3 + chip) * 32, 32), 32)
    my4 = pl.ds(pl.multiple_of(core * 256 + chip * 16, 16), 16)
    far3[my3, :] = jnp.concatenate(sides3, axis=1).astype(BF16)
    far4[my4, :] = jnp.concatenate(sides4, axis=1).astype(BF16)
    far12[96:160, :] = pool12[0:64, :]

    def rows2(row):
        return far12.at[pl.ds(pl.multiple_of(row, 32), 32)]

    own2 = pool12.at[128:160]
    second_far = 1 + 2 * core
    near_copies = [
        remote(own2, rows2(192), near_send, near_recv, 0, later(2)),
        remote(own2, rows2(224 - 64 * core), near_send, near_recv, 1, later(second_far)),
        remote(pool12.at[32:128], far12.at[0:96], near_send, near_recv, 2, later(1)),
    ]
    pass2 = remote(rows2(192), rows2(160 + 64 * core), near_send, near_recv, 3, {"seq": sibling})
    def peer_copies(d):
        return (
            remote(far3.at[my3], far3.at[my3], peer_send, peer_recv, d, {"seq": z_peer(d)}),
            remote(far4.at[my4], far4.at[my4], peer_send, peer_recv, 8 + d, {"seq": z_peer(d)}),
        )

    def line_copies(x, slot, place):
        rows3 = pl.ds(pl.multiple_of(core * STRIDE3 + (BACK3 + x * row_chips) * 32, 32), row_chips * 32)
        rows4 = pl.ds(pl.multiple_of(core * 256 + x * 128, 128), row_chips * 16)
        return (
            remote(far3.at[rows3], far3.at[rows3], side_send, side_recv, slot, place),
            remote(far4.at[rows4], far4.at[rows4], side_send, side_recv, slot + 1, place),
        )

    line_sibling = line_copies(x_low, 0, {"seq": sibling})
    line_next = line_copies(0, 2, {"seq": x_next})
    line_last = line_copies(0, 4, {"seq": sibling})

    for d in range(1, row_chips):
        for copy in peer_copies(d):
            copy.start()
    for copy in near_copies:
        copy.start()
    load_q.wait()
    load_w.start()

    qp[...] = dot_nn(pm[176:240, :], qs[...]).astype(BF16)
    fill_interp(wi)
    fill_masks(pick12, pick3, pick4, s0)

    def near(b, h):
        rows = pl.ds(pl.multiple_of(b * 256, 256), 256)
        next_rows = pl.ds(pl.multiple_of(b * 256 + 256, 256), 256)
        lanes = pl.ds(pl.multiple_of(h * 128, 128), 128)
        vlanes = pl.ds(pl.multiple_of(512 + h * 128, 128), 128)
        q = qs[rows, lanes]
        s_prev = dot_nt(q, kvx[rows, lanes])
        s_own = dot_nt(q, kvx[next_rows, lanes])
        s_prev = jnp.where(s0 + b * 256 > 0, s_prev, BIG)
        s_own = jnp.where(iota((256, 256), 1) <= iota((256, 256), 0), s_own, BIG)
        top = jnp.max(jnp.maximum(s_prev, s_own), axis=1, keepdims=True) * SCALE2
        w_prev = jnp.exp2(s_prev * SCALE2 - top)
        w_own = jnp.exp2(s_own * SCALE2 - top)
        ones = jnp.ones((256, 128), BF16)
        acc = dot_nn(w_prev.astype(BF16), jnp.concatenate([kvx[rows, vlanes], ones], axis=1))
        acc += dot_nn(w_own.astype(BF16), jnp.concatenate([kvx[next_rows, vlanes], ones], axis=1))
        num[rows, lanes] = acc[:, 0:128]
        den[rows, lanes] = acc[:, 128:256]
        mx[rows, lanes] = jnp.broadcast_to(top, (256, 128))

    def near_step(i, carry):
        near(i >> 1, (i & 1) * 2)
        near(i >> 1, (i & 1) * 2 + 1)
        return carry

    w_across(1).start()
    lax.fori_loop(2, 6, near_step, 0)
    for d in range(1, row_chips):
        for copy in peer_copies(d):
            copy.wait_recv()
    for copy in line_sibling:
        copy.start()

    @pl.when(x_low == 0)
    def _():
        for copy in line_next:
            copy.start()

    near_copies[0].wait_recv()
    pass2.start()
    w_across(2).start()
    lax.fori_loop(6, 8, near_step, 0)
    for copy in tail_copies:
        copy.wait_recv()
    lax.fori_loop(0, 2, near_step, 0)
    w_across(3).start()

    @pl.when(x_low == 1)
    def _():
        for copy in line_next:
            copy.wait_recv()
        for copy in line_last:
            copy.start()

    @pl.when(x_low == 0)
    def _():
        for copy in line_next:
            copy.wait_send()

    pass_on(0)
    for copy in line_sibling:
        copy.wait_recv()
    for copy in near_copies[1:] + [pass2]:
        copy.wait_recv()

    @pl.when(x_low == 1)
    def _():
        for copy in line_last:
            copy.wait_recv()

    pass_on(1)

    windows3 = [pl.ds(pl.multiple_of(c * STRIDE3 + chip * 32, 32), 192) for c in range(2)]
    windows4 = [pl.ds(c * 256, 192) for c in range(2)]

    def two(ref, windows, lanes):
        return jnp.concatenate([ref[w, lanes] for w in windows], axis=0)

    def far(h):
        lanes = slice(h * 128, h * 128 + 128)
        vlanes = slice(512 + h * 128, 640 + h * 128)
        keys, values = slice(0, 128), slice(128, 256)
        pooled = qp[:, lanes]
        parts = [
            (pick12[...] > 0, far12[:, lanes], far12[:, vlanes]),
            (pick3[...] == h, two(far3, windows3, keys), two(far3, windows3, values)),
            (pick4[...] == h, two(far4, windows4, keys), two(far4, windows4, values)),
        ]
        scores = [jnp.where(chosen, dot_nt(pooled, key), BIG) for chosen, key, _ in parts]
        top = functools.reduce(jnp.maximum, [jnp.max(s, axis=1, keepdims=True) for s in scores]) * SCALE2
        weights = [
            jnp.where(chosen, jnp.exp2(s * SCALE2 - top), 0.0) for (chosen, _, _), s in zip(parts, scores)
        ]
        total = sum(jnp.sum(w, axis=1, keepdims=True) for w in weights)
        acc = sum(dot_nn(w.astype(BF16), value) for w, (_, _, value) in zip(weights, parts))
        some = total > 0
        safe = jnp.where(some, total, 1.0)
        lse = jnp.where(some, top + jnp.log(safe) * LOG2E, BIG)
        both = jnp.concatenate([acc / safe, jnp.broadcast_to(lse, (64, 128))], axis=1)
        high = both.astype(BF16)
        rest = both - high.astype(F32)
        middle = rest.astype(BF16)
        low = (rest - middle.astype(F32)).astype(BF16)
        for b in range(4):
            for j, part in enumerate((high, middle, low)):
                fo[h * 4 + b, 16 * j : 16 * (j + 1), :] = part[16 * b : 16 * (b + 1), :]

    for h in range(4):
        far(h)

    y_up, y_down, y_far = lax.rem(y + 1, 4), lax.rem(y + 3, 4), lax.rem(y + 2, 4)

    def mix(row):
        rows = pl.ds(pl.multiple_of(row, 128), 128)
        b = lax.div(row, 256)
        weights = wi[pl.ds(pl.multiple_of(lax.rem(row, 256), 128), 128), :]

        for h in range(4):
            lanes = slice(h * 128, h * 128 + 128)
            tok = dot_nn(weights, fo[h * 4 + b])
            tok_out, tok_lse = tok[:, 0:128], tok[:, 128:256]
            near_max = mx[rows, lanes]
            top = jnp.maximum(near_max, tok_lse)
            a = jnp.exp2(near_max - top)
            b_far = jnp.exp2(tok_lse - top)
            mixed = (num[rows, lanes] * a + tok_out * b_far) / (den[rows, lanes] * a + b_far)
            att[rows, lanes] = mixed.astype(BF16)

    def give(target):
        src = pl.ds(pl.multiple_of((1 - half) * 512 + target * 128, 128), 128)
        dst = pl.ds(pl.multiple_of(target * 128, 128), 128)
        return remote(att.at[src], att_in.at[dst], att_send, att_recv, target, {"head": partner})

    def mix_out(target):
        mix((1 - half) * 512 + target * 128)

    def mix_own(target):
        mix(half * 512 + target * 128)

    mix_out(y_far)
    give(y_far).start()
    mix_own(y_far)
    mix_out(y_up)
    give(y_up).start()
    pass_last(0)
    mix_out(y_down)
    mix_own(y_up)
    mix_own(y_down)
    mix_out(y)
    mix_own(y)
    load_w.wait()

    def share(target, chunk):
        own_rows = pl.ds(pl.multiple_of(half * 512 + target * 128, 128), 128)
        in_rows = pl.ds(pl.multiple_of(target * 128, 128), 128)
        cols = pl.ds(pl.multiple_of(chunk * 512, 512), 512)
        return dot_nn(att[own_rows, :], w_own[:, cols]) + dot_nn(att_in[in_rows, :], w_in[:, cols])

    def first_copy(side, j):
        slot = side * 4 + j
        return remote(sb1.at[slot], rb1.at[slot], send1, recv1, slot, {"head": (up, down)[side]})

    def second_copy(side, chunk):
        slot = side * 8 + chunk
        return remote(sb2.at[slot], rb2.at[slot], send2, recv2, slot, {"head": (up, down)[side]})

    def w_ready(j):
        w_sibling(j).wait_recv()
        w_last(j).wait_recv()

    def begin(j, carry):
        for side in range(2):
            sb1[side * 4 + j] = share(y_far, 2 * j + side).astype(BF16)
            first_copy(side, j).start()
        return carry

    def direct(side, j):
        chunk = 2 * j + 1 - side
        sb2[side * 8 + chunk] = share((y_up, y_down)[side], chunk).astype(BF16)
        second_copy(side, chunk).start()

    def direct_up(j, carry):
        direct(0, j)
        return carry

    def direct_down(j, carry):
        direct(1, j)
        return carry

    def follow(j, carry):
        for side in range(2):
            chunk = 2 * j + side
            mine = share((y_up, y_down)[side], chunk)
            first_copy(side, j).wait_recv()
            sb2[side * 8 + chunk] = (mine + rb1[side * 4 + j].astype(F32)).astype(BF16)
            second_copy(side, chunk).start()
        return carry

    give(y_far).wait_send()
    give(y_down).start()
    give(y_far).wait_recv()
    w_ready(0)
    lax.fori_loop(0, 1, begin, 0)
    pass_on(2)
    pass_last(1)
    w_ready(1)
    lax.fori_loop(1, 2, begin, 0)
    give(y_up).wait_send()
    give(y).start()
    give(y_up).wait_recv()
    lax.fori_loop(0, 2, direct_up, 0)
    give(y_down).wait_send()
    give(y_down).wait_recv()
    lax.fori_loop(0, 2, direct_down, 0)
    pass_on(3)
    lax.fori_loop(0, 2, follow, 0)
    pass_last(2)
    w_ready(2)
    lax.fori_loop(2, 3, begin, 0)
    pass_last(3)
    w_ready(3)
    lax.fori_loop(3, 4, begin, 0)
    lax.fori_loop(2, 4, direct_up, 0)
    lax.fori_loop(2, 4, direct_down, 0)
    lax.fori_loop(2, 4, follow, 0)

    give(y).wait_recv()

    def keep(chunk, carry):
        own[chunk] = share(y, chunk)
        return carry

    lax.fori_loop(0, 8, keep, 0)

    def store(chunk):
        cols = pl.ds(pl.multiple_of(chunk * 512, 512), 512)
        return pltpu.make_async_copy(out.at[:, cols], result.at[:, cols], out_sem.at[chunk])

    def finish(chunk, carry):
        for side in range(2):
            second_copy(side, chunk).wait_recv()
        total = own[chunk] + rb2[chunk].astype(F32) + rb2[8 + chunk].astype(F32)
        out[:, pl.ds(pl.multiple_of(chunk * 512, 512), 512)] = total.astype(BF16)
        store(chunk).start()
        return carry

    lax.fori_loop(0, 8, finish, 0)

    for d in range(1, row_chips):
        for copy in peer_copies(d):
            copy.wait_send()
    for copy in near_copies + [pass2] + tail_copies + list(line_sibling):
        copy.wait_send()

    @pl.when(x_low == 1)
    def _():
        for copy in line_last:
            copy.wait_send()

    for j in range(4):
        w_across(j).wait_send()
        w_sibling(j).wait_send()
        w_beside(j).wait_send()
        w_last(j).wait_send()
        for side in range(2):
            first_copy(side, j).wait_send()
            second_copy(side, j).wait_send()
            second_copy(side, 4 + j).wait_send()
    for chunk in range(8):
        store(chunk).wait()
    give(y).wait_send()


def layer(n, q, k, v, w):
    hbm_spec = pl.BlockSpec(memory_space=pltpu.HBM)
    vm = pltpu.VMEM
    return pl.pallas_call(
        functools.partial(kernel, n),
        out_shape=jax.ShapeDtypeStruct((128, 4096), BF16),
        in_specs=[hbm_spec] * 4,
        out_specs=pl.BlockSpec(memory_space=pl.ANY),
        scratch_shapes=[
            vm((1280, 1024), BF16),
            vm((1024, 512), BF16),
            vm((240, 1024), BF16),
            vm((256, 48), BF16),
            vm((176, 1024), F32),
            vm((160, 1024), BF16),
            vm((64, 512), BF16),
            vm((256, 1024), BF16),
            vm((2 * STRIDE3, 256), BF16),
            vm((512, 256), BF16),
            vm((64, 256), jnp.int32),
            vm((64, 384), jnp.int32),
            vm((64, 384), jnp.int32),
            vm((16, 48, 256), BF16),
            vm((1024, 512), F32),
            vm((1024, 512), F32),
            vm((1024, 512), F32),
            vm((1024, 512), BF16),
            vm((512, 512), BF16),
            vm((512, 4096), BF16),
            vm((512, 4096), BF16),
            vm((8, 128, 512), BF16),
            vm((8, 128, 512), BF16),
            vm((16, 128, 512), BF16),
            vm((16, 128, 512), BF16),
            vm((8, 128, 512), F32),
            vm((128, 4096), BF16),
            pltpu.SemaphoreType.DMA((4,)),
        ]
        + [pltpu.SemaphoreType.DMA((count,)) for count in (6, 6, 16, 16, 6, 6, 4, 4, 16, 16, 8, 8, 16, 16, 8)],
        compiler_params=pltpu.CompilerParams(
            collective_id=0, has_side_effects=True, vmem_limit_bytes=52 * 1024 * 1024
        ),
        cost_estimate=pl.CostEstimate(flops=6 * 10**9, bytes_accessed=8 * 2**20, transcendentals=2 * 10**6),
    )(q, k, v, w)


def solution(mesh):
    n = mesh.shape["seq"]

    def body(queries, key_tokens, value_tokens, out_weight):
        return layer(n, queries, key_tokens, value_tokens, out_weight)

    in_specs = (P("seq", "head"), P("seq", "head"), P("seq", "head"), P("head", None))
    out_specs = P(("seq", "head"), None)
    return jax.shard_map(body, mesh=mesh, in_specs=in_specs, out_specs=out_specs, check_vma=False)
```

```python
import functools
import math

import jax
import jax.numpy as jnp
from jax import lax
from jax.experimental import pallas as pl
from jax.experimental.pallas import tpu as pltpu
from jax.sharding import PartitionSpec as P

MESH = pl.DeviceIdType.MESH
HD = 128
BLK = 256
QG = 16
LOG2E = 1.4426950408889634
SCALE2 = LOG2E / math.sqrt(HD)
BIG = -1e30
F32 = jnp.float32
BF16 = jnp.bfloat16

BACK3 = 6
STRIDE3 = 704


def iota(shape, dim):
    return lax.broadcasted_iota(jnp.int32, shape, dim)


def dot_nt(a, b):
    return lax.dot_general(a, b, (((1,), (1,)), ((), ())), preferred_element_type=F32)


def dot_nn(a, b):
    return jnp.dot(a, b, preferred_element_type=F32)


def fill_pool_matrix(pm):
    def piece(rows, shift, weight):
        hit = (iota((rows, 1024), 1) >> shift) == iota((rows, 1024), 0)
        return jnp.where(hit, weight, 0.0).astype(BF16)

    pm[0:128, :] = piece(128, 3, 1.0 / 8)
    pm[128:160, :] = piece(32, 5, 1.0 / 32)
    row, col = iota((16, 1024), 0), iota((16, 1024), 1)
    third = jnp.where((col >> 7) == row, 1.0 / 128, 0.0)
    fourth = jnp.where((col >> 9) == (row & 1), 1.0 / 512, 0.0)
    pm[160:176, :] = jnp.where(row < 8, third, fourth).astype(BF16)
    pm[176:240, :] = piece(64, 4, 1.0 / 16)


def fill_interp(wi):
    row, col = iota((BLK, 48), 0), iota((BLK, 48), 1)
    numer = 2 * row - (QG - 1)
    low = jnp.clip(numer >> 5, 0, BLK // QG - 2)
    frac = jnp.clip((numer - low * 32).astype(F32) * (1.0 / 32), 0.0, 1.0)
    group = col & 15
    value = jnp.where(group == low, 1.0 - frac, 0.0) + jnp.where(group == low + 1, frac, 0.0)
    wi[...] = value.astype(BF16)


def bounds(start):
    first = jnp.maximum(start - 256, 0)
    second = jnp.maximum(((first - 512) >> 5) << 5, 0)
    third = jnp.maximum(((second - 2048) >> 7) << 7, 0)
    fourth = jnp.maximum(((third - 8192) >> 9) << 9, 0)
    return first, second, third, fourth


def fill_masks(pick12, pick3, pick4, s0):
    shape = (64, 256)
    first, second, third, fourth = bounds(s0 + 256 * (iota(shape, 0) >> 4))
    col = iota(shape, 1)
    is_first = col < 160
    token = jnp.where(is_first, s0 - 768 + 8 * col, s0 - 3072 + 32 * (col - 160))
    size = jnp.where(is_first, 8, 32)
    lower = jnp.where(is_first, second, third)
    upper = jnp.where(is_first, first, second)
    pick12[...] = jnp.where((token >= lower) & (token + size <= upper), 1, 0)
    shape = (64, 384)
    first, second, third, fourth = bounds(s0 + 256 * (iota(shape, 0) >> 4))
    col = iota(shape, 1)
    core = jnp.where(col < 192, 0, 1)
    rest = col - 192 * core
    token = ((s0 >> 11) - BACK3 + (rest >> 5)) * 2048 + core * 1024 + (rest & 7) * 128
    chosen = (token >= fourth) & (token + 128 <= third)
    pick3[...] = jnp.where(chosen, (rest & 31) >> 3, -1)
    token = (rest >> 4) * 2048 + core * 1024 + (rest & 1) * 512
    chosen = (token >= 0) & (token + 512 <= fourth)
    pick4[...] = jnp.where(chosen, (rest & 15) >> 1, -1)


def kernel(
    n, q_hbm, k_hbm, v_hbm, w_hbm, result,
    kvx, qs, pm, wi, res, pool12, qp, far12, far3, far4, pick12, pick3, pick4, fo, num, mx, den,
    att, att_in, w_own, w_in, sb1, rb1, sb2, rb2, own, out,
    load_sem, near_send, near_recv, peer_send, peer_recv, side_send, side_recv,
    att_send, att_recv, w_send, w_recv, send1, recv1, send2, recv2, out_sem,
):
    me = lax.axis_index("seq")
    head = lax.axis_index("head")
    s0 = me * 1024
    chips = n // 2
    row_chips = chips // 2
    core = lax.rem(me, 2)
    chip = lax.div(me, 2)
    x_low = lax.div(chip, row_chips)
    z = lax.rem(chip, row_chips)
    half = lax.div(head, 4)
    y = lax.rem(head, 4)
    partner = lax.rem(head + 4, 8)
    up = half * 4 + lax.rem(y + 1, 4)
    down = half * 4 + lax.rem(y + 3, 4)
    x_next = lax.rem(me + chips, n)
    across = {"seq": x_next, "head": partner}
    side_x = x_low * 2 + core
    side_z = lax.rem(me, 4)
    beside_z = me + 2 - 4 * lax.div(side_z, 2)
    sibling = me + 1 - 2 * core

    def z_peer(d):
        return x_low * chips + lax.rem(z + d, row_chips) * 2 + core

    barrier = pltpu.get_barrier_semaphore()
    for c in range(2):
        far3[c * STRIDE3 : c * STRIDE3 + BACK3 * 32, :] = jnp.zeros((BACK3 * 32, 256), BF16)
        far4[c * 256 + 128 : c * 256 + 256, :] = jnp.zeros((128, 256), BF16)
    places = [{"seq": z_peer(d)} for d in range(1, row_chips)]
    places += [{"seq": lax.rem(me + n - k, n)} for k in (1, 2, 3 - 2 * core)]
    places += [{"seq": sibling}, {"seq": x_next}, {"head": partner}, {"head": up}, {"head": down}, across]
    for place in places:
        pl.semaphore_signal(barrier, inc=1, device_id=place, device_id_type=MESH)

    load_k = pltpu.make_async_copy(k_hbm, kvx.at[256:1280, 0:512], load_sem.at[0])
    load_v = pltpu.make_async_copy(v_hbm, kvx.at[256:1280, 512:1024], load_sem.at[1])
    load_q = pltpu.make_async_copy(q_hbm, qs, load_sem.at[2])
    load_w = pltpu.make_async_copy(w_hbm, w_own, load_sem.at[3])
    load_k.start()
    load_v.start()
    load_q.start()

    def remote(src, dst, sends, recvs, slot, place):
        return pltpu.make_async_remote_copy(
            src_ref=src, dst_ref=dst, send_sem=sends.at[slot], recv_sem=recvs.at[slot],
            device_id=place, device_id_type=MESH,
        )

    def later(k):
        return {"seq": lax.rem(me + k, n)}

    def w_copy(src, kind, j, rows_of, place):
        rows = pl.ds(pl.multiple_of(rows_of * 128, 128), 128)
        cols = pl.ds(pl.multiple_of(j * 1024, 1024), 1024)
        return remote(src.at[rows, cols], w_in.at[rows, cols], w_send, w_recv, kind * 4 + j, place)

    def place_of(j):
        return side_z, side_z, beside_z

    def w_across(j):
        return w_copy(w_hbm, 0, j, place_of(j)[1], across)

    def w_sibling(j):
        return w_copy(w_in, 1, j, place_of(j)[0], {"seq": sibling})

    def w_beside(j):
        return w_copy(w_in, 2, j, place_of(j)[0], {"seq": place_of(j)[2]})

    def w_last(j):
        return w_copy(w_in, 3, j, lax.rem(place_of(j)[0] + 2, 4), {"seq": sibling})

    def pass_on(j):
        w_across(j).wait_recv()
        w_sibling(j).start()
        w_beside(j).start()

    def pass_last(j):
        w_beside(j).wait_recv()
        w_last(j).start()

    tail_copies = [
        remote(ref.at[768:1024], kvx.at[0:256, i * 512 : i * 512 + 512], near_send, near_recv, 4 + i, later(1))
        for i, ref in enumerate((k_hbm, v_hbm))
    ]

    fill_pool_matrix(pm)
    pl.semaphore_wait(barrier, len(places))
    for copy in tail_copies:
        copy.start()
    w_across(0).start()

    def pool(c, carry):
        cols = pl.ds(pl.multiple_of(c * 256, 256), 256)
        res[:, cols] = dot_nn(pm[0:176, :], kvx[256:1280, cols])
        return carry

    load_k.wait()
    lax.fori_loop(0, 2, pool, 0)
    load_v.wait()
    lax.fori_loop(2, 4, pool, 0)
    pool12[...] = res[0:160, :].astype(BF16)
    row8 = iota((8, 128), 0)
    sides3, sides4 = [], []
    for side in range(2):
        tiles = [res[160:168, side * 512 + h * 128 : side * 512 + (h + 1) * 128] for h in range(4)]
        last = jnp.zeros((8, 128), F32)
        for h in range(4):
            lanes = slice(side * 512 + h * 128, side * 512 + (h + 1) * 128)
            last = jnp.where((row8 >> 1) == h, res[168:176, lanes], last)
        sides3.append(jnp.concatenate(tiles, axis=0))
        sides4.append(jnp.concatenate([last, jnp.zeros((8, 128), F32)], axis=0))
    my3 = pl.ds(pl.multiple_of(core * STRIDE3 + (BACK3 + chip) * 32, 32), 32)
    my4 = pl.ds(pl.multiple_of(core * 256 + chip * 16, 16), 16)
    far3[my3, :] = jnp.concatenate(sides3, axis=1).astype(BF16)
    far4[my4, :] = jnp.concatenate(sides4, axis=1).astype(BF16)
    far12[96:160, :] = pool12[0:64, :]

    def rows2(row):
        return far12.at[pl.ds(pl.multiple_of(row, 32), 32)]

    own2 = pool12.at[128:160]
    second_far = 1 + 2 * core
    near_copies = [
        remote(own2, rows2(192), near_send, near_recv, 0, later(2)),
        remote(own2, rows2(224 - 64 * core), near_send, near_recv, 1, later(second_far)),
        remote(pool12.at[32:128], far12.at[0:96], near_send, near_recv, 2, later(1)),
    ]
    pass2 = remote(rows2(192), rows2(160 + 64 * core), near_send, near_recv, 3, {"seq": sibling})
    def peer_copies(d):
        return (
            remote(far3.at[my3], far3.at[my3], peer_send, peer_recv, d, {"seq": z_peer(d)}),
            remote(far4.at[my4], far4.at[my4], peer_send, peer_recv, 8 + d, {"seq": z_peer(d)}),
        )

    def line_copies(x, slot, place):
        rows3 = pl.ds(pl.multiple_of(core * STRIDE3 + (BACK3 + x * row_chips) * 32, 32), row_chips * 32)
        rows4 = pl.ds(pl.multiple_of(core * 256 + x * 128, 128), row_chips * 16)
        return (
            remote(far3.at[rows3], far3.at[rows3], side_send, side_recv, slot, place),
            remote(far4.at[rows4], far4.at[rows4], side_send, side_recv, slot + 1, place),
        )

    line_sibling = line_copies(x_low, 0, {"seq": sibling})
    line_next = line_copies(0, 2, {"seq": x_next})
    line_last = line_copies(0, 4, {"seq": sibling})

    for d in range(1, row_chips):
        for copy in peer_copies(d):
            copy.start()
    for copy in near_copies:
        copy.start()
    load_q.wait()
    load_w.start()

    qp[...] = dot_nn(pm[176:240, :], qs[...]).astype(BF16)
    fill_interp(wi)
    fill_masks(pick12, pick3, pick4, s0)

    def near(b, h):
        rows = pl.ds(pl.multiple_of(b * 256, 256), 256)
        next_rows = pl.ds(pl.multiple_of(b * 256 + 256, 256), 256)
        lanes = pl.ds(pl.multiple_of(h * 128, 128), 128)
        vlanes = pl.ds(pl.multiple_of(512 + h * 128, 128), 128)
        q = qs[rows, lanes]
        s_prev = dot_nt(q, kvx[rows, lanes])
        s_own = dot_nt(q, kvx[next_rows, lanes])
        s_prev = jnp.where(s0 + b * 256 > 0, s_prev, BIG)
        s_own = jnp.where(iota((256, 256), 1) <= iota((256, 256), 0), s_own, BIG)
        top = jnp.max(jnp.maximum(s_prev, s_own), axis=1, keepdims=True) * SCALE2
        w_prev = jnp.exp2(s_prev * SCALE2 - top)
        w_own = jnp.exp2(s_own * SCALE2 - top)
        ones = jnp.ones((256, 128), BF16)
        acc = dot_nn(w_prev.astype(BF16), jnp.concatenate([kvx[rows, vlanes], ones], axis=1))
        acc += dot_nn(w_own.astype(BF16), jnp.concatenate([kvx[next_rows, vlanes], ones], axis=1))
        num[rows, lanes] = acc[:, 0:128]
        den[rows, lanes] = acc[:, 128:256]
        mx[rows, lanes] = jnp.broadcast_to(top, (256, 128))

    def near_step(i, carry):
        near(i >> 1, (i & 1) * 2)
        near(i >> 1, (i & 1) * 2 + 1)
        return carry

    w_across(1).start()
    lax.fori_loop(2, 6, near_step, 0)
    for d in range(1, row_chips):
        for copy in peer_copies(d):
            copy.wait_recv()
    for copy in line_sibling:
        copy.start()

    @pl.when(x_low == 0)
    def _():
        for copy in line_next:
            copy.start()

    near_copies[0].wait_recv()
    pass2.start()
    w_across(2).start()
    lax.fori_loop(6, 8, near_step, 0)
    for copy in tail_copies:
        copy.wait_recv()
    lax.fori_loop(0, 2, near_step, 0)
    w_across(3).start()

    @pl.when(x_low == 1)
    def _():
        for copy in line_next:
            copy.wait_recv()
        for copy in line_last:
            copy.start()

    pass_on(0)
    for copy in line_sibling:
        copy.wait_recv()
    for copy in near_copies[1:] + [pass2]:
        copy.wait_recv()

    @pl.when(x_low == 1)
    def _():
        for copy in line_last:
            copy.wait_recv()

    pass_on(1)

    windows3 = [pl.ds(pl.multiple_of(c * STRIDE3 + chip * 32, 32), 192) for c in range(2)]
    windows4 = [pl.ds(c * 256, 192) for c in range(2)]

    def two(ref, windows, lanes):
        return jnp.concatenate([ref[w, lanes] for w in windows], axis=0)

    def far(h):
        lanes = slice(h * 128, h * 128 + 128)
        vlanes = slice(512 + h * 128, 640 + h * 128)
        keys, values = slice(0, 128), slice(128, 256)
        pooled = qp[:, lanes]
        parts = [
            (pick12[...] > 0, far12[:, lanes], far12[:, vlanes]),
            (pick3[...] == h, two(far3, windows3, keys), two(far3, windows3, values)),
            (pick4[...] == h, two(far4, windows4, keys), two(far4, windows4, values)),
        ]
        scores = [jnp.where(chosen, dot_nt(pooled, key), BIG) for chosen, key, _ in parts]
        top = functools.reduce(jnp.maximum, [jnp.max(s, axis=1, keepdims=True) for s in scores]) * SCALE2
        weights = [
            jnp.where(chosen, jnp.exp2(s * SCALE2 - top), 0.0) for (chosen, _, _), s in zip(parts, scores)
        ]
        total = sum(jnp.sum(w, axis=1, keepdims=True) for w in weights)
        acc = sum(dot_nn(w.astype(BF16), value) for w, (_, _, value) in zip(weights, parts))
        some = total > 0
        safe = jnp.where(some, total, 1.0)
        lse = jnp.where(some, top + jnp.log(safe) * LOG2E, BIG)
        both = jnp.concatenate([acc / safe, jnp.broadcast_to(lse, (64, 128))], axis=1)
        high = both.astype(BF16)
        rest = both - high.astype(F32)
        middle = rest.astype(BF16)
        low = (rest - middle.astype(F32)).astype(BF16)
        for b in range(4):
            for j, part in enumerate((high, middle, low)):
                fo[h * 4 + b, 16 * j : 16 * (j + 1), :] = part[16 * b : 16 * (b + 1), :]

    for h in range(4):
        far(h)

    y_up, y_down, y_far = lax.rem(y + 1, 4), lax.rem(y + 3, 4), lax.rem(y + 2, 4)

    def mix(row):
        rows = pl.ds(pl.multiple_of(row, 128), 128)
        b = lax.div(row, 256)
        weights = wi[pl.ds(pl.multiple_of(lax.rem(row, 256), 128), 128), :]

        for h in range(4):
            lanes = slice(h * 128, h * 128 + 128)
            tok = dot_nn(weights, fo[h * 4 + b])
            tok_out, tok_lse = tok[:, 0:128], tok[:, 128:256]
            near_max = mx[rows, lanes]
            top = jnp.maximum(near_max, tok_lse)
            a = jnp.exp2(near_max - top)
            b_far = jnp.exp2(tok_lse - top)
            mixed = (num[rows, lanes] * a + tok_out * b_far) / (den[rows, lanes] * a + b_far)
            att[rows, lanes] = mixed.astype(BF16)

    def give(target):
        src = pl.ds(pl.multiple_of((1 - half) * 512 + target * 128, 128), 128)
        dst = pl.ds(pl.multiple_of(target * 128, 128), 128)
        return remote(att.at[src], att_in.at[dst], att_send, att_recv, target, {"head": partner})

    def mix_out(target):
        mix((1 - half) * 512 + target * 128)

    def mix_own(target):
        mix(half * 512 + target * 128)

    mix_out(y_far)
    give(y_far).start()
    mix_own(y_far)
    mix_out(y_up)
    give(y_up).start()
    mix_out(y_down)
    mix_own(y_up)
    mix_own(y_down)
    mix_out(y)
    mix_own(y)
    pass_last(0)
    load_w.wait()

    def share(target, chunk):
        own_rows = pl.ds(pl.multiple_of(half * 512 + target * 128, 128), 128)
        in_rows = pl.ds(pl.multiple_of(target * 128, 128), 128)
        cols = pl.ds(pl.multiple_of(chunk * 512, 512), 512)
        return dot_nn(att[own_rows, :], w_own[:, cols]) + dot_nn(att_in[in_rows, :], w_in[:, cols])

    def first_copy(side, j):
        slot = side * 4 + j
        return remote(sb1.at[slot], rb1.at[slot], send1, recv1, slot, {"head": (up, down)[side]})

    def second_copy(side, chunk):
        slot = side * 8 + chunk
        return remote(sb2.at[slot], rb2.at[slot], send2, recv2, slot, {"head": (up, down)[side]})

    def w_ready(j):
        w_sibling(j).wait_recv()
        w_last(j).wait_recv()

    def begin(j, carry):
        for side in range(2):
            sb1[side * 4 + j] = share(y_far, 2 * j + side).astype(BF16)
            first_copy(side, j).start()
        return carry

    def direct(side, j):
        chunk = 2 * j + 1 - side
        sb2[side * 8 + chunk] = share((y_up, y_down)[side], chunk).astype(BF16)
        second_copy(side, chunk).start()

    def direct_up(j, carry):
        direct(0, j)
        return carry

    def direct_down(j, carry):
        direct(1, j)
        return carry

    def follow(j, carry):
        for side in range(2):
            chunk = 2 * j + side
            mine = share((y_up, y_down)[side], chunk)
            first_copy(side, j).wait_recv()
            sb2[side * 8 + chunk] = (mine + rb1[side * 4 + j].astype(F32)).astype(BF16)
            second_copy(side, chunk).start()
        return carry

    give(y_far).wait_send()
    give(y_down).start()
    give(y_far).wait_recv()
    w_ready(0)
    lax.fori_loop(0, 1, begin, 0)
    pass_last(1)
    w_ready(1)
    lax.fori_loop(1, 2, begin, 0)
    pass_on(2)
    give(y_up).wait_send()
    give(y).start()
    give(y_up).wait_recv()
    lax.fori_loop(0, 2, direct_up, 0)
    give(y_down).wait_send()
    give(y_down).wait_recv()
    lax.fori_loop(0, 2, direct_down, 0)
    pass_on(3)
    lax.fori_loop(0, 2, follow, 0)
    pass_last(2)
    w_ready(2)
    lax.fori_loop(2, 3, begin, 0)
    pass_last(3)
    w_ready(3)
    lax.fori_loop(3, 4, begin, 0)
    lax.fori_loop(2, 4, direct_up, 0)
    lax.fori_loop(2, 4, direct_down, 0)
    lax.fori_loop(2, 4, follow, 0)

    give(y).wait_recv()

    def keep(chunk, carry):
        own[chunk] = share(y, chunk)
        return carry

    lax.fori_loop(0, 8, keep, 0)

    def store(chunk):
        cols = pl.ds(pl.multiple_of(chunk * 512, 512), 512)
        return pltpu.make_async_copy(out.at[:, cols], result.at[:, cols], out_sem.at[chunk])

    def finish(chunk, carry):
        for side in range(2):
            second_copy(side, chunk).wait_recv()
        total = own[chunk] + rb2[chunk].astype(F32) + rb2[8 + chunk].astype(F32)
        out[:, pl.ds(pl.multiple_of(chunk * 512, 512), 512)] = total.astype(BF16)
        store(chunk).start()
        return carry

    lax.fori_loop(0, 8, finish, 0)

    for d in range(1, row_chips):
        for copy in peer_copies(d):
            copy.wait_send()
    for copy in near_copies + [pass2] + tail_copies + list(line_sibling):
        copy.wait_send()

    @pl.when(x_low == 0)
    def _():
        for copy in line_next:
            copy.wait_send()

    @pl.when(x_low == 1)
    def _():
        for copy in line_last:
            copy.wait_send()

    for j in range(4):
        w_across(j).wait_send()
        w_sibling(j).wait_send()
        w_beside(j).wait_send()
        w_last(j).wait_send()
        for side in range(2):
            first_copy(side, j).wait_send()
            second_copy(side, j).wait_send()
            second_copy(side, 4 + j).wait_send()
    for chunk in range(8):
        store(chunk).wait()
    give(y).wait_send()


def layer(n, q, k, v, w):
    hbm_spec = pl.BlockSpec(memory_space=pltpu.HBM)
    vm = pltpu.VMEM
    return pl.pallas_call(
        functools.partial(kernel, n),
        out_shape=jax.ShapeDtypeStruct((128, 4096), BF16),
        in_specs=[hbm_spec] * 4,
        out_specs=pl.BlockSpec(memory_space=pl.ANY),
        scratch_shapes=[
            vm((1280, 1024), BF16),
            vm((1024, 512), BF16),
            vm((240, 1024), BF16),
            vm((256, 48), BF16),
            vm((176, 1024), F32),
            vm((160, 1024), BF16),
            vm((64, 512), BF16),
            vm((256, 1024), BF16),
            vm((2 * STRIDE3, 256), BF16),
            vm((512, 256), BF16),
            vm((64, 256), jnp.int32),
            vm((64, 384), jnp.int32),
            vm((64, 384), jnp.int32),
            vm((16, 48, 256), BF16),
            vm((1024, 512), F32),
            vm((1024, 512), F32),
            vm((1024, 512), F32),
            vm((1024, 512), BF16),
            vm((512, 512), BF16),
            vm((512, 4096), BF16),
            vm((512, 4096), BF16),
            vm((8, 128, 512), BF16),
            vm((8, 128, 512), BF16),
            vm((16, 128, 512), BF16),
            vm((16, 128, 512), BF16),
            vm((8, 128, 512), F32),
            vm((128, 4096), BF16),
            pltpu.SemaphoreType.DMA((4,)),
        ]
        + [pltpu.SemaphoreType.DMA((count,)) for count in (6, 6, 16, 16, 6, 6, 4, 4, 16, 16, 8, 8, 16, 16, 8)],
        compiler_params=pltpu.CompilerParams(
            collective_id=0, has_side_effects=True, vmem_limit_bytes=52 * 1024 * 1024
        ),
        cost_estimate=pl.CostEstimate(flops=6 * 10**9, bytes_accessed=8 * 2**20, transcendentals=2 * 10**6),
    )(q, k, v, w)


def solution(mesh):
    n = mesh.shape["seq"]

    def body(queries, key_tokens, value_tokens, out_weight):
        return layer(n, queries, key_tokens, value_tokens, out_weight)

    in_specs = (P("seq", "head"), P("seq", "head"), P("seq", "head"), P("head", None))
    out_specs = P(("seq", "head"), None)
    return jax.shard_map(body, mesh=mesh, in_specs=in_specs, out_specs=out_specs, check_vma=False)
```
